512 devices in a mesh: dp: 64 (over y_lo, z, core), tensor: 8 (over x, y_hi).
Axes of the slice: x: 4, y: 4 (y_hi: 2, y_lo: 2; y = y_hi * 2 + y_lo), z: 16, core: 2. Of those that a mesh axis runs over, the one named last changes fastest.
Arguments:
- resp_q: bfloat16 [8192, 8192], P(('dp', 'tensor')), may hold values from -8 to 8
- resp_kv: bfloat16 [8192, 2048], P(('dp', 'tensor')), may hold values from -6 to 6
- prompt_kv: bfloat16 [2048, 2048], P('dp', 'tensor'), may hold values from -6 to 6
- grad_out: bfloat16 [8192, 8192], P(('dp', 'tensor')), may hold values from -6 to 6
- lengths: int32 [128], replicated, may hold values from 8 to 64, as said below
- resp_lists: int32 [64, 2], replicated, may hold values from 0 to 127, as said below
- owner_map: int32 [64], replicated, may hold values from 0 to 63, each once
Outputs:
- attention: bfloat16 [8192, 8192], P(('dp', 'tensor'))
- query_grad: bfloat16 [8192, 8192], P(('dp', 'tensor'))
- response_grad: bfloat16 [8192, 2048], P(('dp', 'tensor'))
- prompt_grad: bfloat16 [2048, 2048], P('dp', 'tensor')
The draws below stay inside these ranges and needn't reach their ends.
Inputs may be any that keep to these rules, and one draw needn't show every extreme that they name: `lengths`: some response has 8 tokens and some has 64. `resp_lists`: every response appears in exactly one slot.
All inputs are finite; a program needn't handle non-finite values.
Results may differ from the reference program's by a relative error of at most 0.02.
Values may be sent and summed in bfloat16 or wider, within the bound.
A program may use at most 64 MiB of HBM per device.

```python
import math
import jax
import jax.numpy as jnp
from jax import lax

HQ = 64
KVH = 8
HD = 128
BLOCKS = 8
G = 16
PL = 256
LR = 64
PROMPTS = 8
RESP = 128
TOT_ROWS = 8192
PTOK = 2048
N_DP = 64


def paired_lengths(key):
    key = jax.random.fold_in(key, 11)
    first_key, second_key = jax.random.split(key)
    base = jax.random.randint(first_key, (RESP,), LR // 8, LR + 1)
    order = jax.random.permutation(second_key, RESP)
    iota_rows = jnp.arange(RESP)
    base = jnp.where(iota_rows == order[0], LR, base)
    base = jnp.where(iota_rows == order[1], LR // 8, base)
    return base.astype(jnp.int32)


def draw_lengths(key, part):
    return paired_lengths(key)


def draw_resp_lists(key, part):
    resp_lengths = paired_lengths(key)
    order = jnp.argsort(resp_lengths, stable=True).astype(jnp.int32)
    learners = RESP // 2
    longer = order[::-1][:learners]
    shorter = order[:learners]
    return jnp.stack([longer, shorter], 1).astype(jnp.int32)


def draw_resp_q(key, part):
    key = jax.random.fold_in(key, 3)
    first_key = jax.random.fold_in(key, 0)
    base = jax.random.normal(first_key, (TOT_ROWS, HQ * HD), jnp.float32)
    base = jnp.clip(base, -6.0, 6.0)
    return base.astype(jnp.bfloat16)


def draw_prompt_kv(key, part):
    key = jax.random.fold_in(key, 5)
    base = jnp.clip(jax.random.normal(key, (PTOK, KVH, 2, HD), jnp.float32), -6.0, 6.0)
    return base.reshape(PTOK, KVH * 2 * HD).astype(jnp.bfloat16)


def level_of(rng, dims, pieces, smallest, high):
    level = 1.0
    for dim, shards_of in pieces:
        draws = jax.random.uniform(jax.random.fold_in(jax.random.fold_in(rng, 6), dim), (shards_of,), jnp.float32, smallest / len(pieces), high / len(pieces))
        level = level * jnp.repeat(jnp.exp(draws), dims[dim] // shards_of).reshape((-1,) + (1,) * (len(dims) - 1 - dim))
    return level


def normal_values(own_key, shape, scale, reach, cuts=(), kind=jnp.bfloat16):
    array = jax.random.normal(own_key, shape, jnp.float32) * scale
    if len(cuts) > 0:
        array = level_of(own_key, shape, cuts, -0.22, 0.18) * array
    return jnp.clip(array, min=-reach, max=reach).astype(kind)


def setup_inputs(seed: int = 0) -> dict:
    keys = jax.random.split(jax.random.key(seed), 8)
    return {
        "resp_q": draw_resp_q(jax.random.fold_in(keys[7], 71), 0),
        "resp_kv": normal_values(keys[1], (TOT_ROWS, KVH * 2 * HD), 1.0, 6.0, ((0, 512),)),
        "prompt_kv": draw_prompt_kv(jax.random.fold_in(keys[7], 71), 0),
        "grad_out": normal_values(keys[3], (TOT_ROWS, HQ * HD), 1.0, 6.0, ((0, 512),)),
        "lengths": draw_lengths(jax.random.fold_in(keys[7], 71), 0),
        "resp_lists": draw_resp_lists(jax.random.fold_in(keys[7], 71), 0),
        "owner_map": jax.random.permutation(keys[6], N_DP).astype(jnp.int32),
    }


def rounded(values):
    return lax.optimization_barrier(values.astype(jnp.bfloat16)).astype(jnp.float32)

def attend_learner(query_rows, own_rows, grad_rows, chosen, resp_lengths, prompt_table):
    scale_factor = 1.0 / math.sqrt(HD)
    slot_count = chosen.shape[0]
    group_size = HQ // KVH
    prompt_ids = chosen // G
    positions = jnp.arange(LR)
    live_rows = positions[None, :] < jnp.take(resp_lengths, chosen)[:, None]
    live_mask = live_rows.astype(jnp.float32)
    query = query_rows.reshape(slot_count, LR, KVH, group_size, HD).astype(jnp.float32)
    own_kv = own_rows.reshape(slot_count, LR, KVH, 2, HD).astype(jnp.float32)
    cotangent = grad_rows.reshape(slot_count, LR, KVH, group_size, HD).astype(jnp.float32) * live_mask[:, :, None, None, None]
    picked = prompt_table[prompt_ids].astype(jnp.float32)
    prompt_keys = picked[:, :, :, 0]
    prompt_values = picked[:, :, :, 1]
    own_keys = own_kv[:, :, :, 0]
    own_values = own_kv[:, :, :, 1]
    prompt_scores = jnp.einsum('sthgd,skhd->sthgk', query, prompt_keys) * scale_factor
    own_scores = jnp.einsum('sthgd,suhd->sthgu', query, own_keys) * scale_factor
    allowed = (positions[None, :] <= positions[:, None])[None] & live_rows[:, None, :]
    own_scores = jnp.where(allowed[:, :, None, None, :], own_scores, -jnp.inf)
    row_max = jnp.maximum(prompt_scores.max(-1), own_scores.max(-1))
    prompt_exp = jnp.exp(prompt_scores - row_max[..., None])
    own_exp = jnp.exp(own_scores - row_max[..., None])
    row_total = prompt_exp.sum(-1) + own_exp.sum(-1)
    prompt_probs = prompt_exp / row_total[..., None]
    own_probs = own_exp / row_total[..., None]
    prompt_rounded = rounded(prompt_probs)
    own_rounded = rounded(own_probs)
    mixed = jnp.einsum('sthgk,skhd->sthgd', prompt_rounded, prompt_values) + jnp.einsum('sthgu,suhd->sthgd', own_rounded, own_values)
    attention = (mixed * live_mask[:, :, None, None, None]).astype(jnp.bfloat16)
    delta = lax.optimization_barrier(jnp.sum(cotangent * attention.astype(jnp.float32), -1))
    prompt_dprob = jnp.einsum('sthgd,skhd->sthgk', cotangent, prompt_values)
    own_dprob = jnp.einsum('sthgd,suhd->sthgu', cotangent, own_values)
    prompt_ds = rounded(scale_factor * prompt_probs * (prompt_dprob - delta[..., None]))
    own_ds = rounded(scale_factor * own_probs * (own_dprob - delta[..., None]))
    query_grad = (jnp.einsum('sthgk,skhd->sthgd', prompt_ds, prompt_keys) + jnp.einsum('sthgu,suhd->sthgd', own_ds, own_keys)).astype(jnp.bfloat16)
    own_dk = jnp.einsum('sthgu,sthgd->suhd', own_ds, query)
    own_dv = jnp.einsum('sthgu,sthgd->suhd', own_rounded, cotangent)
    response_grad = jnp.stack([own_dk, own_dv], 3).astype(jnp.bfloat16)
    prompt_dk = jnp.einsum('sthgk,sthgd->skhd', prompt_ds, query)
    prompt_dv = jnp.einsum('sthgk,sthgd->skhd', prompt_rounded, cotangent)
    prompt_terms = jnp.stack([prompt_dk, prompt_dv], 3)
    return (attention, query_grad, response_grad, prompt_terms, prompt_ids)

def reference(resp_q, resp_kv, prompt_kv, grad_out, lengths, resp_lists, owner_map):
    learners = resp_lists.shape[0]
    slot_count = resp_lists.shape[1]
    block_rows = PL // BLOCKS
    row_width = KVH * 2 * HD
    rows_each = slot_count * LR
    inverse = jnp.argsort(owner_map).astype(jnp.int32)
    prompt_table = prompt_kv.reshape(learners, block_rows, row_width)[inverse].reshape(PROMPTS, PL, KVH, 2, HD)

    def learner_step(owner_table, inputs):
        query_rows, own_rows, grad_rows, chosen = inputs
        attention, query_grad, response_grad, prompt_terms, prompt_ids = attend_learner(query_rows, own_rows, grad_rows, chosen, lengths, prompt_table)
        for slot_index in range(slot_count):
            owner_table = owner_table.at[prompt_ids[slot_index]].add(prompt_terms[slot_index])
        return (owner_table, (attention, query_grad, response_grad))
    empty_table = jnp.zeros((PROMPTS, PL, KVH, 2, HD), jnp.float32)
    inputs = (resp_q.reshape(learners, rows_each, HQ * HD), resp_kv.reshape(learners, rows_each, row_width), grad_out.reshape(learners, rows_each, HQ * HD), resp_lists)
    owner_table, results = lax.scan(learner_step, empty_table, inputs)
    attention = results[0].reshape(TOT_ROWS, HQ * HD)
    query_grad = results[1].reshape(TOT_ROWS, HQ * HD)
    response_grad = results[2].reshape(TOT_ROWS, row_width)
    prompt_grad = owner_table.reshape(PROMPTS * BLOCKS, block_rows, row_width)[owner_map].reshape(PTOK, row_width).astype(jnp.bfloat16)
    return (attention, query_grad, response_grad, prompt_grad)
```

```python
import math

import jax
import jax.numpy as jnp
from jax import lax
from jax.experimental import pallas as pl
from jax.experimental.pallas import tpu as pltpu
from jax.sharding import PartitionSpec as P

MESH = pl.DeviceIdType.MESH
BF = jnp.bfloat16
F32 = jnp.float32
HD = 128
BLOCKS = 8
G = 16
Z = 16
T = 8
SLOTS = 2
LR = 64
GROUP = 8
BR = 32
PL = BLOCKS * BR
KEYS = PL + LR
HW = GROUP * HD
KW = 2 * HD
SCALE = 1.0 / math.sqrt(HD)
NEAR = (4, -4, 3, -3, 2, -2, 1, -1)


def dot(a, b, dims):
    return lax.dot_general(a, b, (dims, ((), ())), preferred_element_type=F32)


def kernel(
    q_in, kv_in, pkv_in, g_in, lengths, lists, owners,
    att_out, qg_out, rg_out, pg_out,
    qbuf, gbuf, kvbuf, obuf, dqbuf, rgbuf,
    table, kcat, vcat, probs_t, dscore_t,
    compact, part, direct, relay_a, relay_b, relayed, rsum, ysum,
    loc_sem, a2a_s, a2a_r, agz_s, agz_r, agy_s, agy_r, agc_s, agc_r,
    back_s, back_r, cc_s, cc_r, rs_s, rs_r, fy_s, fy_r,
):
    dp = lax.axis_index("dp")
    t = lax.axis_index("tensor")
    core = lax.rem(dp, 2)
    z = lax.rem(dp // 2, Z)
    y = dp // (2 * Z)

    def at_z(d):
        return (y * (2 * Z) + lax.rem(z + d + Z, Z) * 2 + core, t)

    other_core = (y * (2 * Z) + z * 2 + (1 - core), t)
    other_y = ((1 - y) * (2 * Z) + z * 2 + core, t)
    peers = [(lax.rem(t + k, T)) for k in range(1, T)]

    def remote(src, dst, s, r, device):
        return pltpu.make_async_remote_copy(
            src_ref=src, dst_ref=dst, send_sem=s, recv_sem=r, device_id=device, device_id_type=MESH
        )

    def columns(width, index):
        return pl.ds(pl.multiple_of(index * width, width), width)

    local = [
        pltpu.make_async_copy(pkv_in, table.at[0, 0, 8], loc_sem.at[0]),
        pltpu.make_async_copy(q_in.at[:, columns(HW, t)], qbuf.at[t], loc_sem.at[1]),
        pltpu.make_async_copy(g_in.at[:, columns(HW, t)], gbuf.at[t], loc_sem.at[2]),
        pltpu.make_async_copy(kv_in.at[:, columns(KW, t)], kvbuf.at[t], loc_sem.at[3]),
    ]
    for copy in local:
        copy.start()
    barrier = pltpu.get_barrier_semaphore()
    greeted = [at_z(d) for d in NEAR] + [other_core, other_y] + [(dp, p) for p in peers]
    for device in greeted:
        pl.semaphore_signal(barrier, inc=1, device_id=device, device_id_type=MESH)
    pl.semaphore_wait(barrier, len(greeted))

    def gather(slot, d):
        dst_slot = slot - d
        src = pkv_in if slot == 8 else table.at[0, 0, slot]
        return remote(src, table.at[0, 0, dst_slot], agz_s.at[dst_slot], agz_r.at[dst_slot], at_z(d))

    sends = []
    step1 = {d: gather(8, d) for d in NEAR}
    for d in NEAR:
        step1[d].start()
        sends.append(step1[d])

    a2a = []
    for i, p in enumerate(peers):
        for a, (src, dst, width) in enumerate(((kv_in, kvbuf, KW), (q_in, qbuf, HW), (g_in, gbuf, HW))):
            copy = remote(src.at[:, columns(width, p)], dst.at[t], a2a_s.at[a, i], a2a_r.at[a, i], (dp, p))
            copy.start()
            a2a.append(copy)

    resp = [lists[dp, s] for s in range(SLOTS)]
    prompt = [lax.div(a, G) for a in resp]
    length = [lengths[a] for a in resp]

    def find(j, found):
        code = owners[j]
        return tuple(
            jnp.where(code == prompt[s] * BLOCKS + b, j, found[s * BLOCKS + b])
            for s in range(SLOTS)
            for b in range(BLOCKS)
        )

    found = lax.fori_loop(0, 4 * Z, find, tuple(jnp.int32(0) for _ in range(SLOTS * BLOCKS)))

    step1[4].wait_recv()
    for d in (4, 3, 2, 1):
        copy = gather(4, d)
        copy.start()
        sends.append(copy)
    step1[-4].wait_recv()
    for d in (-3, -2, -1):
        copy = gather(12, d)
        copy.start()
        sends.append(copy)
    local[0].wait()
    ranges = (pl.ds(4, 9), pl.ds(0, 4), pl.ds(13, 3))
    over_y = [
        remote(table.at[0, 0, r], table.at[1, 0, r], agy_s.at[i], agy_r.at[i], other_y)
        for i, r in enumerate(ranges)
    ]
    over_core = [
        [
            remote(table.at[a, 0, r], table.at[a, 1, r], agc_s.at[a, i], agc_r.at[a, i], other_core)
            for i, r in enumerate(ranges)
        ]
        for a in range(2)
    ]
    for d in NEAR[2:]:
        step1[d].wait_recv()
    over_y[0].start()
    over_core[0][0].start()
    for i, slots in ((1, (3, 2, 1, 0)), (2, (13, 14, 15))):
        for slot in slots:
            gather(slot, 0).wait_recv()
        over_y[i].start()
        over_core[0][i].start()
    for i in range(3):
        over_y[i].wait_recv()
        over_core[1][i].start()
    for copy in local[1:]:
        copy.wait()
    for copy in a2a:
        copy.wait_recv()
    for i in range(3):
        over_core[0][i].wait_recv()
    for i in range(3):
        over_core[1][i].wait_recv()

    def stacked(buf, s, first, heads):
        cols = [buf[4 * s : 4 * s + 4, :, pl.ds(pl.multiple_of(first + h * HD, HD), HD)].reshape(LR, HD) for h in range(heads)]
        return jnp.concatenate(cols, axis=0)

    half = GROUP // 2
    wide = half * LR
    for s in range(SLOTS):
        n = length[s]
        row = lax.broadcasted_iota(jnp.int32, (LR, HW), 0)
        masked = jnp.where(row < n, gbuf[4 * s : 4 * s + 4].reshape(LR, HW).astype(F32), 0.0)
        gbuf[4 * s : 4 * s + 4] = masked.astype(BF).reshape(4, 16, HW)
        for b in range(BLOCKS):
            j = found[s * BLOCKS + b]
            jy, jz, jc = lax.div(j, 2 * Z), lax.rem(lax.div(j, 2), Z), lax.rem(j, 2)
            block = table[jnp.where(jy == y, 0, 1), jnp.where(jc == core, 0, 1), lax.rem(jz - z + 8 + Z, Z)]
            kcat[b * BR : (b + 1) * BR] = block[:, :HD]
            vcat[b * BR : (b + 1) * BR] = block[:, HD:]
        own = kvbuf[4 * s : 4 * s + 4].reshape(LR, KW)
        kcat[PL:] = own[:, :HD]
        vcat[PL:] = own[:, HD:]
        keys, values = kcat[...], vcat[...]

        def part_of(h, _, s=s, n=n, keys=keys, values=values):
            q = stacked(qbuf, s, h * half * HD, half)
            g = stacked(gbuf, s, h * half * HD, half)
            scores = dot(keys, q, ((1,), (1,))) * SCALE
            u = lax.broadcasted_iota(jnp.int32, (LR, wide), 0)
            at = lax.rem(lax.broadcasted_iota(jnp.int32, (LR, wide), 1), LR)
            own_scores = jnp.where((u <= at) & (u < n), scores[PL:], -jnp.inf)
            scores = jnp.concatenate([scores[:PL], own_scores], axis=0)
            top = jnp.max(scores, axis=0, keepdims=True)
            e = jnp.exp(scores - top)
            probs = e * (1.0 / jnp.sum(e, axis=0, keepdims=True))
            rounded = probs.astype(BF)
            dprob = dot(values, g, ((1,), (1,)))
            delta = jnp.sum(rounded.astype(F32) * dprob, axis=0, keepdims=True)
            dscore = (probs * (dprob - delta) * SCALE).astype(BF)
            at_cols = pl.ds(pl.multiple_of(h * wide, wide), wide)
            probs_t[:, at_cols] = rounded
            dscore_t[:, at_cols] = dscore
            out = dot(rounded, values, ((0,), (0,)))
            dq = dot(dscore, keys, ((0,), (0,)))
            live = lax.broadcasted_iota(jnp.int32, (LR, HD), 0) < n
            for i in range(half):
                head = pl.ds(pl.multiple_of(h * half * HD + i * HD, HD), HD)
                rows = slice(i * LR, (i + 1) * LR)
                obuf[4 * s : 4 * s + 4, :, head] = jnp.where(live, out[rows], 0.0).astype(BF).reshape(4, 16, HD)
                dqbuf[4 * s : 4 * s + 4, :, head] = dq[rows].astype(BF).reshape(4, 16, HD)
            return 0

        lax.fori_loop(0, 2, part_of, 0)
        dk = dot(dscore_t[...], stacked(qbuf, s, 0, GROUP), ((1,), (0,)))
        dv = dot(probs_t[...], stacked(gbuf, s, 0, GROUP), ((1,), (0,)))
        both = jnp.concatenate([dk, dv], axis=1).astype(BF)
        for b in range(BLOCKS):
            compact[0, s, b] = both[b * BR : (b + 1) * BR]
        rgbuf[4 * s : 4 * s + 4] = both[PL:].reshape(4, 16, KW)
        copy = remote(compact.at[0, s], compact.at[1, s], cc_s.at[s], cc_r.at[s], other_core)
        copy.start()
        sends.append(copy)

    back = []
    for i, p in enumerate(peers):
        for a, (src, dst_ref, width) in enumerate(((obuf, att_out, HW), (dqbuf, qg_out, HW), (rgbuf, rg_out, KW))):
            copy = remote(src.at[p], dst_ref.at[:, columns(width, t)], back_s.at[a, i], back_r.at[a, i], (dp, p))
            copy.start()
            back.append(copy)
    stay = [
        pltpu.make_async_copy(src.at[t], dst_ref.at[:, columns(width, t)], loc_sem.at[4 + a])
        for a, (src, dst_ref, width) in enumerate(((obuf, att_out, HW), (dqbuf, qg_out, HW), (rgbuf, rg_out, KW)))
    ]
    for copy in stay:
        copy.start()

    for s in range(SLOTS):
        remote(compact.at[0, s], compact.at[1, s], cc_s.at[s], cc_r.at[s], other_core).wait_recv()
    learner2 = dp + 1 - 2 * core
    slot_prompts = prompt + [lax.div(lists[learner2, s], G) for s in range(SLOTS)]

    def fill(k, _):
        for yy in range(2):
            code = owners[yy * (2 * Z) + lax.rem(z + k + 8, Z) * 2 + core]
            p, b = lax.div(code, BLOCKS), lax.rem(code, BLOCKS)
            total = jnp.zeros((BR, KW), F32)
            for c in range(2):
                for s in range(SLOTS):
                    hit = slot_prompts[c * SLOTS + s] == p
                    total = total + jnp.where(hit, compact[c, s, b].astype(F32), 0.0)
            part[k, yy] = total.astype(BF)
        return 0

    lax.fori_loop(0, Z, fill, 0)

    rs = []

    def rs_send(i, src, dst_ref, d):
        copy = remote(src, dst_ref, rs_s.at[i], rs_r.at[i], at_z(d))
        copy.start()
        rs.append(copy)
        sends.append(copy)

    for i, d in enumerate((4, 3, 2, 1)):
        rs_send(i, part.at[(8 + d + 4) % Z], relay_a.at[i], d)
    for i, d in enumerate((-3, -2, -1)):
        rs_send(4 + i, part.at[8 + d - 4], relay_b.at[i], d)
    for i, d in enumerate((3, -3, 2, -2, 1, -1)):
        rs_send(7 + i, part.at[8 + d], direct.at[i], d)
    for copy in rs[:4]:
        copy.wait_recv()
    total = part[12].astype(F32)
    for i in range(4):
        total = total + relay_a[i].astype(F32)
    part[12] = total.astype(BF)
    rs_send(13, part.at[12], relayed.at[0], 4)
    for copy in rs[4:7]:
        copy.wait_recv()
    total = part[4].astype(F32)
    for i in range(3):
        total = total + relay_b[i].astype(F32)
    part[4] = total.astype(BF)
    rs_send(14, part.at[4], relayed.at[1], -4)
    for copy in rs[7:13]:
        copy.wait_recv()
    total = part[8].astype(F32)
    for i in range(6):
        total = total + direct[i].astype(F32)
    for i in range(2):
        rs[13 + i].wait_recv()
        total = total + relayed[i].astype(F32)
    rsum[...] = total
    copy = remote(rsum.at[1 - y], ysum, fy_s.at[0], fy_r.at[0], other_y)
    copy.start()
    sends.append(copy)
    copy.wait_recv()
    pg_out[...] = (rsum[y] + ysum[...]).astype(BF)

    for copy in back:
        copy.wait_recv()
    for copy in stay:
        copy.wait()
    for copy in sends + a2a + back + over_y + over_core[0] + over_core[1]:
        copy.wait_send()


def on_device(resp_q, resp_kv, prompt_kv, grad_out, lengths, resp_lists, owner_map):
    anywhere = pl.BlockSpec(memory_space=pl.ANY)
    scalars = pl.BlockSpec(memory_space=pltpu.SMEM)
    rows = resp_q.shape[0]
    dma = pltpu.SemaphoreType.DMA
    return pl.pallas_call(
        kernel,
        name="attention",
        out_shape=(
            jax.ShapeDtypeStruct(resp_q.shape, BF),
            jax.ShapeDtypeStruct(resp_q.shape, BF),
            jax.ShapeDtypeStruct(resp_kv.shape, BF),
            jax.ShapeDtypeStruct(prompt_kv.shape, BF),
        ),
        in_specs=[anywhere, anywhere, anywhere, anywhere, scalars, scalars, scalars],
        out_specs=(anywhere, anywhere, anywhere, pl.BlockSpec(memory_space=pltpu.VMEM)),
        scratch_shapes=[
            pltpu.VMEM((T, rows, HW), BF),
            pltpu.VMEM((T, rows, HW), BF),
            pltpu.VMEM((T, rows, KW), BF),
            pltpu.VMEM((T, rows, HW), BF),
            pltpu.VMEM((T, rows, HW), BF),
            pltpu.VMEM((T, rows, KW), BF),
            pltpu.VMEM((2, 2, Z, BR, KW), BF),
            pltpu.VMEM((KEYS, HD), BF),
            pltpu.VMEM((KEYS, HD), BF),
            pltpu.VMEM((KEYS, GROUP * LR), BF),
            pltpu.VMEM((KEYS, GROUP * LR), BF),
            pltpu.VMEM((2, SLOTS, BLOCKS, BR, KW), BF),
            pltpu.VMEM((Z, 2, BR, KW), BF),
            pltpu.VMEM((6, 2, BR, KW), BF),
            pltpu.VMEM((4, 2, BR, KW), BF),
            pltpu.VMEM((3, 2, BR, KW), BF),
            pltpu.VMEM((2, 2, BR, KW), BF),
            pltpu.VMEM((2, BR, KW), F32),
            pltpu.VMEM((BR, KW), F32),
            dma((7,)),
            dma((3, T - 1)),
            dma((3, T - 1)),
            dma((Z,)),
            dma((Z,)),
            dma((3,)),
            dma((3,)),
            dma((2, 3)),
            dma((2, 3)),
            dma((3, T - 1)),
            dma((3, T - 1)),
            dma((SLOTS,)),
            dma((SLOTS,)),
            dma((15,)),
            dma((15,)),
            dma((1,)),
            dma((1,)),
        ],
        compiler_params=pltpu.CompilerParams(
            collective_id=0, has_side_effects=True, vmem_limit_bytes=40 * 1024 * 1024
        ),
    )(resp_q, resp_kv, prompt_kv, grad_out, lengths, resp_lists, owner_map)


def solution(mesh):
    rows = P(("dp", "tensor"), None)
    return jax.shard_map(
        on_device,
        mesh=mesh,
        in_specs=(rows, rows, P("dp", "tensor"), rows, P(), P(), P()),
        out_specs=(rows, rows, rows, P("dp", "tensor")),
        check_vma=False,
    )
```

```python
import math

import jax
import jax.numpy as jnp
from jax import lax
from jax.experimental import pallas as pl
from jax.experimental.pallas import tpu as pltpu
from jax.sharding import PartitionSpec as P

MESH = pl.DeviceIdType.MESH
BF = jnp.bfloat16
F32 = jnp.float32
HD = 128
BLOCKS = 8
G = 16
Z = 16
T = 8
SLOTS = 2
LR = 64
GROUP = 8
BR = 32
PL = BLOCKS * BR
KEYS = PL + LR
HW = GROUP * HD
KW = 2 * HD
HALF = GROUP // 2
WIDE = HALF * LR
SCALE = 1.0 / math.sqrt(HD)
NEAR = (4, -4, 3, -3, 2, -2, 1, -1)
K, V = 0, 1


def dot(a, b, dims):
    return lax.dot_general(a, b, (dims, ((), ())), preferred_element_type=F32)


def kernel(
    q_in, kv_in, pkv_in, g_in, lengths_in, lists_in, owners_in,
    att_out, qg_out, rg_out, pg_out,
    qbuf, gbuf, kvbuf, obuf, dqbuf, rgbuf,
    table_k, table_v, kcat, vcat, probs_f, probs_t, dscore_t,
    compact_k, compact_v, part, direct, relay_a, relay_b, relayed, rsum, ysum, lengths, lists, owners,
    loc, a2a_s, a2a_r, agz_s, agz_r, agy_s, agy_r, agc_s, agc_r, back_s, back_r, cc_s, cc_r, rs_s, rs_r, fy_s, fy_r,
):
    table, compact = (table_k, table_v), (compact_k, compact_v)
    dp = lax.axis_index("dp")
    t = lax.axis_index("tensor")
    core = lax.rem(dp, 2)
    z = lax.rem(dp // 2, Z)
    y = dp // (2 * Z)

    def at_z(d):
        return (y * (2 * Z) + lax.rem(z + d + Z, Z) * 2 + core, t)

    other_core = (y * (2 * Z) + z * 2 + (1 - core), t)
    other_y = ((1 - y) * (2 * Z) + z * 2 + core, t)
    peers = [lax.rem(t + k, T) for k in range(1, T)]

    def send(src, dst, s, r, device):
        pltpu.make_async_remote_copy(
            src_ref=src, dst_ref=dst, send_sem=s, recv_sem=r, device_id=device, device_id_type=MESH
        ).start()

    def wait(ref, sem):
        pltpu.make_async_copy(ref, ref, sem).wait()

    def columns(width, index):
        return pl.ds(pl.multiple_of(index * width, width), width)

    barrier = pltpu.get_barrier_semaphore()
    greeted = [(dp, p) for p in peers] + [at_z(d) for d in NEAR] + [other_y, other_core]
    for device in greeted:
        pl.semaphore_signal(barrier, inc=1, device_id=device, device_id_type=MESH)
    local = [
        pltpu.make_async_copy(pkv_in.at[:, :HD], table[K].at[0, 0, 8], loc.at[0]),
        pltpu.make_async_copy(pkv_in.at[:, HD:], table[V].at[0, 0, 8], loc.at[1]),
        pltpu.make_async_copy(kv_in.at[:, columns(KW, t)], kvbuf.at[t], loc.at[2]),
        pltpu.make_async_copy(q_in.at[:, columns(HW, t)], qbuf.at[t], loc.at[3]),
        pltpu.make_async_copy(g_in.at[:, columns(HW, t)], gbuf.at[t], loc.at[4]),
        pltpu.make_async_copy(lengths_in, lengths, loc.at[5]),
        pltpu.make_async_copy(lists_in, lists, loc.at[6]),
        pltpu.make_async_copy(owners_in, owners, loc.at[7]),
    ]
    for copy in local:
        copy.start()
    for copy in local[:2]:
        copy.wait()
    pl.semaphore_wait(barrier, len(greeted))

    def arrival(slot):
        return 0 if slot == 4 else 1 if slot == 12 else 2 if 4 < slot < 12 else 3 if slot < 4 else 4

    def gather(kv, slot, d):
        to = slot - d
        send(table[kv].at[0, 0, slot], table[kv].at[0, 0, to], agz_s.at[kv], agz_r.at[kv, arrival(to)], at_z(d))

    def to_heads(a, src, dst, width):
        for p in peers:
            send(src.at[:, columns(width, p)], dst.at[t], a2a_s.at[a], a2a_r.at[a], (dp, p))

    for d in NEAR:
        gather(K, 8, d)
    to_heads(0, kv_in, kvbuf, KW)
    for d in NEAR:
        gather(V, 8, d)
    to_heads(1, q_in, qbuf, HW)
    to_heads(2, g_in, gbuf, HW)

    for kv in (K, V):
        wait(table[kv].at[0, 0, 4], agz_r.at[kv, 0])
        for d in (4, 3, 2, 1):
            gather(kv, 4, d)
        wait(table[kv].at[0, 0, 12], agz_r.at[kv, 1])
        for d in (-3, -2, -1):
            gather(kv, 12, d)

    groups = (pl.ds(4, 9), pl.ds(0, 4), pl.ds(13, 3))

    def over_y(kv, i):
        r = groups[i]
        send(table[kv].at[0, 0, r], table[kv].at[1, 0, r], agy_s.at[kv], agy_r.at[kv, i], other_y)

    def over_core(kv, a, i):
        r = groups[i]
        send(table[kv].at[a, 0, r], table[kv].at[a, 1, r], agc_s.at[kv], agc_r.at[kv], other_core)

    for kv in (K, V):
        wait(table[kv].at[0, 0, pl.ds(4, 6)], agz_r.at[kv, 2])
        over_y(kv, 0)
        over_core(kv, 0, 0)

    for copy in local[5:]:
        copy.wait()
    resp = [lists[s, dp] for s in range(SLOTS)]
    prompt = [lax.div(a, G) for a in resp]
    length = [lengths[a] for a in resp]

    def find(j, found):
        code = owners[j]
        return tuple(
            jnp.where(code == prompt[s] * BLOCKS + b, j, found[s * BLOCKS + b])
            for s in range(SLOTS)
            for b in range(BLOCKS)
        )

    found = lax.fori_loop(0, 4 * Z, find, tuple(jnp.int32(0) for _ in range(SLOTS * BLOCKS)), unroll=4)

    def pick(cat, kv, s):
        for b in range(BLOCKS):
            j = found[s * BLOCKS + b]
            jy, jz, jc = lax.div(j, 2 * Z), lax.rem(lax.div(j, 2), Z), lax.rem(j, 2)
            block = table[kv][jnp.where(jy == y, 0, 1), jnp.where(jc == core, 0, 1), lax.rem(jz - z + 8 + Z, Z)]
            cat[s, b * BR : (b + 1) * BR] = block

    for kv in (K, V):
        for i in (1, 2):
            wait(table[kv].at[0, 0, groups[i]], agz_r.at[kv, 2 + i])
            over_y(kv, i)
            over_core(kv, 0, i)
    for kv in (K, V):
        for i in range(3):
            wait(table[kv].at[1, 0, groups[i]], agy_r.at[kv, i])
            over_core(kv, 1, i)
    for copy in local[2:5]:
        copy.wait()
    for a, buf in enumerate((kvbuf, qbuf, gbuf)):
        wait(buf.at[pl.ds(0, T - 1)], a2a_r.at[a])
    for s in range(SLOTS):
        row = lax.broadcasted_iota(jnp.int32, (LR, HW), 0)
        masked = jnp.where(row < length[s], gbuf[4 * s : 4 * s + 4].reshape(LR, HW).astype(F32), 0.0)
        gbuf[4 * s : 4 * s + 4] = masked.astype(BF).reshape(4, 16, HW)
        own = kvbuf[4 * s : 4 * s + 4].reshape(LR, KW)
        kcat[s, PL:] = own[:, :HD]
        vcat[s, PL:] = own[:, HD:]

    def stacked(buf, s, first, heads):
        cols = [buf[4 * s : 4 * s + 4, :, pl.ds(pl.multiple_of(first + h * HD, HD), HD)].reshape(LR, HD) for h in range(heads)]
        return jnp.concatenate(cols, axis=0)

    def hand_over(kv, s, grad):
        out = grad.astype(BF)
        compact[kv][0, s] = out[:PL].reshape(BLOCKS, BR, HD)
        rgbuf[4 * s : 4 * s + 4, :, kv * HD : (kv + 1) * HD] = out[PL:].reshape(4, 16, HD)
        send(compact[kv].at[0, s], compact[kv].at[1, s], cc_s.at[kv], cc_r.at[kv], other_core)

    wait(table[K].at[:, 1], agc_r.at[K])
    for s in range(SLOTS):
        pick(kcat, K, s)
        n, keys = length[s], kcat[s]

        def first_pass(h, _, s=s, n=n, keys=keys):
            q = stacked(qbuf, s, h * HALF * HD, HALF)
            scores = dot(keys, q, ((1,), (1,))) * SCALE
            u = lax.broadcasted_iota(jnp.int32, (LR, WIDE), 0)
            at = lax.rem(lax.broadcasted_iota(jnp.int32, (LR, WIDE), 1), LR)
            own_scores = jnp.where((u <= at) & (u < n), scores[PL:], -jnp.inf)
            scores = jnp.concatenate([scores[:PL], own_scores], axis=0)
            top = jnp.max(scores, axis=0, keepdims=True)
            e = jnp.exp(scores - top)
            probs = e * (1.0 / jnp.sum(e, axis=0, keepdims=True))
            cols = columns(WIDE, h)
            probs_f[s, :, cols] = probs
            probs_t[s, :, cols] = probs.astype(BF)
            return 0

        lax.fori_loop(0, 2, first_pass, 0)
        hand_over(V, s, dot(probs_t[s], stacked(gbuf, s, 0, GROUP), ((1,), (0,))))

    learner2 = dp + 1 - 2 * core
    slot_prompts = prompt + [lax.div(lists[s, learner2], G) for s in range(SLOTS)]

    def fill(kv, first, count):
        def one(i, _):
            k = lax.rem(first + i, Z)
            for a in range(2):
                code = owners[(y + a - 2 * a * y) * (2 * Z) + lax.rem(z + k + 8, Z) * 2 + core]
                p, b = lax.div(code, BLOCKS), lax.rem(code, BLOCKS)
                total = jnp.zeros((BR, HD), F32)
                for c in range(2):
                    for s in range(SLOTS):
                        hit = slot_prompts[c * SLOTS + s] == p
                        total = total + jnp.where(hit, compact[kv][c, s, b].astype(F32), 0.0)
                part[kv, k, a] = total.astype(BF)
            return 0

        lax.fori_loop(0, count, one, 0)

    def set_out(kv):
        wait(compact[kv].at[1], cc_r.at[kv])
        fill(kv, 13, 4)
        for i, d in enumerate((4, 3, 2, 1)):
            send(part.at[kv, (8 + d + 4) % Z], relay_a.at[kv, i], rs_s.at[0], rs_r.at[kv, 0], at_z(d))
        fill(kv, 1, 3)
        for i, d in enumerate((-3, -2, -1)):
            send(part.at[kv, 8 + d - 4], relay_b.at[kv, i], rs_s.at[0], rs_r.at[kv, 1], at_z(d))
        fill(kv, 4, 9)
        for i, d in enumerate(NEAR[2:]):
            send(part.at[kv, 8 + d], direct.at[kv, i], rs_s.at[0], rs_r.at[kv, 2], at_z(d))

    def relay(kv):
        for j, (slot, buf, count) in enumerate(((12, relay_a, 4), (4, relay_b, 3))):
            wait(buf.at[kv], rs_r.at[kv, j])
            total = part[kv, slot].astype(F32)
            for i in range(count):
                total = total + buf[kv, i].astype(F32)
            part[kv, slot] = total.astype(BF)
            send(part.at[kv, slot], relayed.at[kv, j], rs_s.at[0], rs_r.at[kv, 3], at_z(slot - 8))

    def to_other_y(kv):
        wait(direct.at[kv], rs_r.at[kv, 2])
        total = part[kv, 8].astype(F32)
        for i in range(6):
            total = total + direct[kv, i].astype(F32)
        wait(relayed.at[kv], rs_r.at[kv, 3])
        for i in range(2):
            total = total + relayed[kv, i].astype(F32)
        rsum[kv] = total
        send(rsum.at[kv, 1], ysum.at[kv], fy_s.at[0], fy_r.at[kv], other_y)

    wait(table[V].at[:, 1], agc_r.at[V])
    for s in range(SLOTS):
        pick(vcat, V, s)
        n, keys, values = length[s], kcat[s], vcat[s]

        def second_pass(h, _, s=s, n=n, keys=keys, values=values):
            g = stacked(gbuf, s, h * HALF * HD, HALF)
            cols = columns(WIDE, h)
            rounded = probs_t[s, :, cols]
            dprob = dot(values, g, ((1,), (1,)))
            delta = jnp.sum(rounded.astype(F32) * dprob, axis=0, keepdims=True)
            dscore = (probs_f[s, :, cols] * (dprob - delta) * SCALE).astype(BF)
            dscore_t[:, cols] = dscore
            out = dot(rounded, values, ((0,), (0,)))
            dq = dot(dscore, keys, ((0,), (0,)))
            live = lax.broadcasted_iota(jnp.int32, (LR, HD), 0) < n
            for i in range(HALF):
                head = pl.ds(pl.multiple_of(h * HALF * HD + i * HD, HD), HD)
                rows = slice(i * LR, (i + 1) * LR)
                obuf[4 * s : 4 * s + 4, :, head] = jnp.where(live, out[rows], 0.0).astype(BF).reshape(4, 16, HD)
                dqbuf[4 * s : 4 * s + 4, :, head] = dq[rows].astype(BF).reshape(4, 16, HD)
            return 0

        lax.fori_loop(0, 2, second_pass, 0)
        hand_over(K, s, dot(dscore_t[...], stacked(qbuf, s, 0, GROUP), ((1,), (0,))))
        if s == 0:
            set_out(V)

    set_out(K)
    relay(V)

    results = ((obuf, att_out, HW), (dqbuf, qg_out, HW), (rgbuf, rg_out, KW))
    for a, (src, to, width) in enumerate(results):
        for p in peers:
            send(src.at[p], to.at[:, columns(width, t)], back_s.at[a], back_r.at[a], (dp, p))
    stay = [
        pltpu.make_async_copy(src.at[t], to.at[:, columns(width, t)], loc.at[a])
        for a, (src, to, width) in enumerate(results)
    ]
    for copy in stay:
        copy.start()

    relay(K)
    to_other_y(V)
    to_other_y(K)
    for kv in (V, K):
        wait(ysum.at[kv], fy_r.at[kv])
        pg_out[:, kv * HD : (kv + 1) * HD] = (rsum[kv, 0] + ysum[kv]).astype(BF)

    for a, (buf, _, _) in enumerate(results):
        wait(buf.at[pl.ds(0, T - 1)], back_r.at[a])
        wait(buf.at[pl.ds(0, T - 1)], back_s.at[a])
    for copy in stay:
        copy.wait()
    for a, buf in enumerate((kvbuf, qbuf, gbuf)):
        wait(buf.at[pl.ds(0, T - 1)], a2a_s.at[a])
    for kv in (K, V):
        wait(table[kv].at[0, 0, pl.ds(0, 15)], agz_s.at[kv])
        wait(table[kv].at[0, 0], agy_s.at[kv])
        wait(table[kv].at[:, 0], agc_s.at[kv])
        wait(compact[kv].at[0], cc_s.at[kv])
    wait(part.at[:, pl.ds(0, 15)], rs_s.at[0])
    wait(ysum, fy_s.at[0])


def hand_on(*refs):
    sem = refs[8]
    copies = [pltpu.make_async_copy(refs[i], refs[4 + i], sem.at[i]) for i in range(4)]
    for copy in copies:
        copy.start()
    for copy in copies:
        copy.wait()


def on_device(resp_q, resp_kv, prompt_kv, grad_out, lengths, resp_lists, owner_map):
    anywhere = pl.BlockSpec(memory_space=pl.ANY)
    in_vmem = pl.BlockSpec(memory_space=pltpu.VMEM)
    rows = resp_q.shape[0]
    dma = pltpu.SemaphoreType.DMA
    results = pl.pallas_call(
        kernel,
        name="attention",
        out_shape=(
            jax.ShapeDtypeStruct(resp_q.shape, BF),
            jax.ShapeDtypeStruct(resp_q.shape, BF),
            jax.ShapeDtypeStruct(resp_kv.shape, BF),
            jax.ShapeDtypeStruct(prompt_kv.shape, BF),
        ),
        in_specs=[anywhere] * 7,
        out_specs=(anywhere, anywhere, anywhere, in_vmem),
        scratch_shapes=[
            pltpu.VMEM((T, rows, HW), BF),
            pltpu.VMEM((T, rows, HW), BF),
            pltpu.VMEM((T, rows, KW), BF),
            pltpu.VMEM((T, rows, HW), BF),
            pltpu.VMEM((T, rows, HW), BF),
            pltpu.VMEM((T, rows, KW), BF),
            pltpu.VMEM((2, 2, Z, BR, HD), BF),
            pltpu.VMEM((2, 2, Z, BR, HD), BF),
            pltpu.VMEM((SLOTS, KEYS, HD), BF),
            pltpu.VMEM((SLOTS, KEYS, HD), BF),
            pltpu.VMEM((SLOTS, KEYS, GROUP * LR), F32),
            pltpu.VMEM((SLOTS, KEYS, GROUP * LR), BF),
            pltpu.VMEM((KEYS, GROUP * LR), BF),
            pltpu.VMEM((2, SLOTS, BLOCKS, BR, HD), BF),
            pltpu.VMEM((2, SLOTS, BLOCKS, BR, HD), BF),
            pltpu.VMEM((2, Z, 2, BR, HD), BF),
            pltpu.VMEM((2, 6, 2, BR, HD), BF),
            pltpu.VMEM((2, 4, 2, BR, HD), BF),
            pltpu.VMEM((2, 3, 2, BR, HD), BF),
            pltpu.VMEM((2, 2, 2, BR, HD), BF),
            pltpu.VMEM((2, 2, BR, HD), F32),
            pltpu.VMEM((2, BR, HD), F32),
            pltpu.SMEM(lengths.shape, jnp.int32),
            pltpu.SMEM(resp_lists.shape[::-1], jnp.int32),
            pltpu.SMEM(owner_map.shape, jnp.int32),
            dma((8,)),
            dma((3,)),
            dma((3,)),
            dma((2,)),
            dma((2, 5)),
            dma((2,)),
            dma((2, 3)),
            dma((2,)),
            dma((2,)),
            dma((3,)),
            dma((3,)),
            dma((2,)),
            dma((2,)),
            dma((1,)),
            dma((2, 4)),
            dma((1,)),
            dma((2,)),
        ],
        compiler_params=pltpu.CompilerParams(
            collective_id=0, has_side_effects=True, vmem_limit_bytes=60 * 1024 * 1024
        ),
    )(resp_q, resp_kv, prompt_kv, grad_out, lengths, resp_lists.T, owner_map)
    return pl.pallas_call(
        hand_on,
        name="hand_on",
        out_shape=tuple(jax.ShapeDtypeStruct(r.shape, r.dtype) for r in results),
        in_specs=[in_vmem] * 4,
        out_specs=(anywhere,) * 4,
        scratch_shapes=[dma((4,))],
    )(*results)


def solution(mesh):
    rows = P(("dp", "tensor"), None)
    return jax.shard_map(
        on_device,
        mesh=mesh,
        in_specs=(rows, rows, P("dp", "tensor"), rows, P(), P(), P()),
        out_specs=(rows, rows, rows, P("dp", "tensor")),
        check_vma=False,
    )
```

```python
import math

import jax
import jax.numpy as jnp
from jax import lax
from jax.experimental import pallas as pl
from jax.experimental.pallas import tpu as pltpu
from jax.sharding import PartitionSpec as P

MESH = pl.DeviceIdType.MESH
BF = jnp.bfloat16
F32 = jnp.float32
HD = 128
BLOCKS = 8
G = 16
Z = 16
T = 8
SLOTS = 2
LR = 64
GROUP = 8
BR = 32
PL = BLOCKS * BR
KEYS = PL + LR
HW = GROUP * HD
KW = 2 * HD
HALF = GROUP // 2
WIDE = HALF * LR
SCALE = 1.0 / math.sqrt(HD)
NEAR = (4, -4, 3, -3, 2, -2, 1, -1)
DIRECT = tuple((a, d) for d in NEAR[2:] for a in (1, 0)) + ((1, 0),)
K, V = 0, 1


def dot(a, b, dims):
    return lax.dot_general(a, b, (dims, ((), ())), preferred_element_type=F32)


def kernel(
    q_in, kv_in, pkv_in, g_in, lengths_in, lists_in, owners_in,
    att_out, qg_out, rg_out, pg_out,
    qbuf, gbuf, kvbuf, obuf, dqbuf, rgbuf,
    table_k, table_v, kcat, vcat, probs_f, probs_t, dscore_t,
    compact_k, compact_v, part, direct, relay_a, relay_b, relayed, lengths, lists, owners,
    loc, a2a_s, a2a_r, agz_s, agz_r, agy_s, agy_r, agc_s, agc_r, back_s, back_r, cc_s, cc_r, rs_s, rs_r,
):
    table, compact = (table_k, table_v), (compact_k, compact_v)
    dp = lax.axis_index("dp")
    t = lax.axis_index("tensor")
    core = lax.rem(dp, 2)
    z = lax.rem(dp // 2, Z)
    y = dp // (2 * Z)

    def at(a, d):
        return ((y + a - 2 * a * y) * (2 * Z) + lax.rem(z + d + Z, Z) * 2 + core, t)

    other_core = (y * (2 * Z) + z * 2 + (1 - core), t)
    peers = [lax.rem(t + k, T) for k in range(1, T)]

    def send(src, dst, s, r, device):
        pltpu.make_async_remote_copy(
            src_ref=src, dst_ref=dst, send_sem=s, recv_sem=r, device_id=device, device_id_type=MESH
        ).start()

    def wait(ref, sem):
        pltpu.make_async_copy(ref, ref, sem).wait()

    def columns(width, index):
        return pl.ds(pl.multiple_of(index * width, width), width)

    barrier = pltpu.get_barrier_semaphore()
    greeted = [(dp, p) for p in peers] + [at(a, d) for d in NEAR for a in (1, 0)] + [at(1, 0), other_core]
    for device in greeted:
        pl.semaphore_signal(barrier, inc=1, device_id=device, device_id_type=MESH)
    local = [
        pltpu.make_async_copy(pkv_in.at[:, :HD], table[K].at[0, 0, 8], loc.at[0]),
        pltpu.make_async_copy(pkv_in.at[:, HD:], table[V].at[0, 0, 8], loc.at[1]),
        pltpu.make_async_copy(kv_in.at[:, columns(KW, t)], kvbuf.at[t], loc.at[2]),
        pltpu.make_async_copy(q_in.at[:, columns(HW, t)], qbuf.at[t], loc.at[3]),
        pltpu.make_async_copy(g_in.at[:, columns(HW, t)], gbuf.at[t], loc.at[4]),
        pltpu.make_async_copy(lengths_in, lengths, loc.at[5]),
        pltpu.make_async_copy(lists_in, lists, loc.at[6]),
        pltpu.make_async_copy(owners_in, owners, loc.at[7]),
    ]
    for copy in local:
        copy.start()
    for copy in local[:2]:
        copy.wait()
    pl.semaphore_wait(barrier, len(greeted))

    def arrival(a, slot):
        return 0 if slot == 4 else 1 if slot == 12 else 2 if 4 < slot < 12 else 3 + 2 * a if slot < 4 else 4 + 2 * a

    def gather(kv, a, slot, d):
        to = slot - d
        send(table[kv].at[0, 0, slot], table[kv].at[a, 0, to], agz_s.at[kv], agz_r.at[kv, arrival(a, to)], at(a, d))

    def to_heads(a, src, dst, width):
        for p in peers:
            send(src.at[:, columns(width, p)], dst.at[t], a2a_s.at[a], a2a_r.at[a], (dp, p))

    for d in NEAR:
        gather(K, 0, 8, d)
    to_heads(0, kv_in, kvbuf, KW)
    for d in NEAR:
        gather(V, 0, 8, d)
    to_heads(1, q_in, qbuf, HW)
    to_heads(2, g_in, gbuf, HW)

    for kv in (K, V):
        wait(table[kv].at[0, 0, 4], agz_r.at[kv, 0])
        for d in (4, 3, 2, 1):
            for a in (1, 0):
                gather(kv, a, 4, d)
        wait(table[kv].at[0, 0, 12], agz_r.at[kv, 1])
        for d in (-3, -2, -1):
            for a in (1, 0):
                gather(kv, a, 12, d)

    groups = (pl.ds(4, 9), pl.ds(0, 4), pl.ds(13, 3))

    def over_core(kv, a, i):
        r = groups[i]
        send(table[kv].at[a, 0, r], table[kv].at[a, 1, r], agc_s.at[kv], agc_r.at[kv], other_core)

    for kv in (K, V):
        wait(table[kv].at[0, 0, pl.ds(4, 6)], agz_r.at[kv, 2])
        near = groups[0]
        send(table[kv].at[0, 0, near], table[kv].at[1, 0, near], agy_s.at[kv], agy_r.at[kv], at(1, 0))
        over_core(kv, 0, 0)

    for copy in local[5:]:
        copy.wait()
    resp = [lists[s, dp] for s in range(SLOTS)]
    prompt = [lax.div(a, G) for a in resp]
    length = [lengths[a] for a in resp]

    def find(j, found):
        code = owners[j]
        return tuple(
            jnp.where(code == prompt[s] * BLOCKS + b, j, found[s * BLOCKS + b])
            for s in range(SLOTS)
            for b in range(BLOCKS)
        )

    found = lax.fori_loop(0, 4 * Z, find, tuple(jnp.int32(0) for _ in range(SLOTS * BLOCKS)), unroll=4)

    def pick(cat, kv, s):
        for b in range(BLOCKS):
            j = found[s * BLOCKS + b]
            jy, jz, jc = lax.div(j, 2 * Z), lax.rem(lax.div(j, 2), Z), lax.rem(j, 2)
            block = table[kv][jnp.where(jy == y, 0, 1), jnp.where(jc == core, 0, 1), lax.rem(jz - z + 8 + Z, Z)]
            cat[s, b * BR : (b + 1) * BR] = block

    for kv in (K, V):
        wait(table[kv].at[1, 0, groups[0]], agy_r.at[kv])
        over_core(kv, 1, 0)
        for i in (1, 2):
            for a in range(2):
                wait(table[kv].at[a, 0, groups[i]], agz_r.at[kv, 2 + i + 2 * a])
                over_core(kv, a, i)
    for copy in local[2:5]:
        copy.wait()
    for a, buf in enumerate((kvbuf, qbuf, gbuf)):
        wait(buf.at[pl.ds(0, T - 1)], a2a_r.at[a])
    for s in range(SLOTS):
        row = lax.broadcasted_iota(jnp.int32, (LR, HW), 0)
        masked = jnp.where(row < length[s], gbuf[4 * s : 4 * s + 4].reshape(LR, HW).astype(F32), 0.0)
        gbuf[4 * s : 4 * s + 4] = masked.astype(BF).reshape(4, 16, HW)
        own = kvbuf[4 * s : 4 * s + 4].reshape(LR, KW)
        kcat[s, PL:] = own[:, :HD]
        vcat[s, PL:] = own[:, HD:]

    def stacked(buf, s, first, heads):
        cols = [buf[4 * s : 4 * s + 4, :, pl.ds(pl.multiple_of(first + h * HD, HD), HD)].reshape(LR, HD) for h in range(heads)]
        return jnp.concatenate(cols, axis=0)

    def hand_over(kv, s, grad):
        out = grad.astype(BF)
        compact[kv][0, s] = out[:PL].reshape(BLOCKS, BR, HD)
        rgbuf[4 * s : 4 * s + 4, :, kv * HD : (kv + 1) * HD] = out[PL:].reshape(4, 16, HD)
        send(compact[kv].at[0, s], compact[kv].at[1, s], cc_s.at[kv], cc_r.at[kv], other_core)

    wait(table[K].at[:, 1], agc_r.at[K])
    for s in range(SLOTS):
        pick(kcat, K, s)
        n, keys = length[s], kcat[s]

        def first_pass(h, _, s=s, n=n, keys=keys):
            q = stacked(qbuf, s, h * HALF * HD, HALF)
            scores = dot(keys, q, ((1,), (1,))) * SCALE
            u = lax.broadcasted_iota(jnp.int32, (LR, WIDE), 0)
            at = lax.rem(lax.broadcasted_iota(jnp.int32, (LR, WIDE), 1), LR)
            own_scores = jnp.where((u <= at) & (u < n), scores[PL:], -jnp.inf)
            scores = jnp.concatenate([scores[:PL], own_scores], axis=0)
            top = jnp.max(scores, axis=0, keepdims=True)
            e = jnp.exp(scores - top)
            probs = e * (1.0 / jnp.sum(e, axis=0, keepdims=True))
            cols = columns(WIDE, h)
            probs_f[s, :, cols] = probs
            probs_t[s, :, cols] = probs.astype(BF)
            return 0

        lax.fori_loop(0, 2, first_pass, 0, unroll=True)
        hand_over(V, s, dot(probs_t[s], stacked(gbuf, s, 0, GROUP), ((1,), (0,))))

    learner2 = dp + 1 - 2 * core
    slot_prompts = prompt + [lax.div(lists[s, learner2], G) for s in range(SLOTS)]

    def fill(kv, first, count):
        def one(i, _):
            k = lax.rem(first + i, Z)
            for a in range(2):
                code = owners[(y + a - 2 * a * y) * (2 * Z) + lax.rem(z + k + 8, Z) * 2 + core]
                p, b = lax.div(code, BLOCKS), lax.rem(code, BLOCKS)
                total = jnp.zeros((BR, HD), F32)
                for c in range(2):
                    for s in range(SLOTS):
                        hit = slot_prompts[c * SLOTS + s] == p
                        total = total + jnp.where(hit, compact[kv][c, s, b].astype(F32), 0.0)
                part[kv, k, a] = total.astype(BF)
            return 0

        lax.fori_loop(0, count, one, 0)

    def set_out(kv):
        wait(compact[kv].at[1], cc_r.at[kv])
        fill(kv, 13, 4)
        for i, d in enumerate((4, 3, 2, 1)):
            send(part.at[kv, (8 + d + 4) % Z], relay_a.at[kv, i], rs_s.at[kv, 0], rs_r.at[kv, 0], at(0, d))
        fill(kv, 1, 3)
        for i, d in enumerate((-3, -2, -1)):
            send(part.at[kv, 8 + d - 4], relay_b.at[kv, i], rs_s.at[kv, 0], rs_r.at[kv, 1], at(0, d))
        fill(kv, 4, 9)
        for i, (a, d) in enumerate(DIRECT):
            send(part.at[kv, 8 + d, a], direct.at[kv, i], rs_s.at[kv, 1], rs_r.at[kv, 2], at(a, d))

    def relay(kv):
        for j, (slot, buf, count) in enumerate(((12, relay_a, 4), (4, relay_b, 3))):
            wait(buf.at[kv], rs_r.at[kv, j])
            total = part[kv, slot].astype(F32)
            for i in range(count):
                total = total + buf[kv, i].astype(F32)
            part[kv, slot] = total.astype(BF)
            for a in (1, 0):
                send(part.at[kv, slot, a], relayed.at[kv, 2 * j + a], rs_s.at[kv, 2], rs_r.at[kv, 3], at(a, slot - 8))

    def finish(kv):
        wait(direct.at[kv], rs_r.at[kv, 2])
        total = part[kv, 8, 0].astype(F32)
        for i in range(len(DIRECT)):
            total = total + direct[kv, i].astype(F32)
        wait(relayed.at[kv], rs_r.at[kv, 3])
        for i in range(4):
            total = total + relayed[kv, i].astype(F32)
        pg_out[:, kv * HD : (kv + 1) * HD] = total.astype(BF)

    wait(table[V].at[:, 1], agc_r.at[V])
    for s in range(SLOTS):
        pick(vcat, V, s)
        n, keys, values = length[s], kcat[s], vcat[s]

        def second_pass(h, _, s=s, n=n, keys=keys, values=values):
            g = stacked(gbuf, s, h * HALF * HD, HALF)
            cols = columns(WIDE, h)
            rounded = probs_t[s, :, cols]
            dprob = dot(values, g, ((1,), (1,)))
            delta = jnp.sum(rounded.astype(F32) * dprob, axis=0, keepdims=True)
            dscore = (probs_f[s, :, cols] * (dprob - delta) * SCALE).astype(BF)
            dscore_t[:, cols] = dscore
            out = dot(rounded, values, ((0,), (0,)))
            dq = dot(dscore, keys, ((0,), (0,)))
            live = lax.broadcasted_iota(jnp.int32, (LR, HD), 0) < n
            for i in range(HALF):
                head = pl.ds(pl.multiple_of(h * HALF * HD + i * HD, HD), HD)
                rows = slice(i * LR, (i + 1) * LR)
                obuf[4 * s : 4 * s + 4, :, head] = jnp.where(live, out[rows], 0.0).astype(BF).reshape(4, 16, HD)
                dqbuf[4 * s : 4 * s + 4, :, head] = dq[rows].astype(BF).reshape(4, 16, HD)
            return 0

        lax.fori_loop(0, 2, second_pass, 0, unroll=True)
        hand_over(K, s, dot(dscore_t[...], stacked(qbuf, s, 0, GROUP), ((1,), (0,))))
        if s == 0:
            set_out(V)

    set_out(K)
    relay(V)

    results = ((obuf, att_out, HW), (dqbuf, qg_out, HW), (rgbuf, rg_out, KW))
    for a, (src, to, width) in enumerate(results):
        for p in peers:
            send(src.at[p], to.at[:, columns(width, t)], back_s.at[a], back_r.at[a], (dp, p))
    stay = [
        pltpu.make_async_copy(src.at[t], to.at[:, columns(width, t)], loc.at[a])
        for a, (src, to, width) in enumerate(results)
    ]
    for copy in stay:
        copy.start()

    relay(K)
    finish(V)
    finish(K)

    for a, (buf, _, _) in enumerate(results):
        wait(buf.at[pl.ds(0, T - 1)], back_r.at[a])
        wait(buf.at[pl.ds(0, T - 1)], back_s.at[a])
    for copy in stay:
        copy.wait()
    for a, buf in enumerate((kvbuf, qbuf, gbuf)):
        wait(buf.at[pl.ds(0, T - 1)], a2a_s.at[a])
    for kv in (K, V):
        wait(table[kv].at[:, 0, pl.ds(0, 11)], agz_s.at[kv])
        wait(table[kv].at[0, 0, near], agy_s.at[kv])
        wait(table[kv].at[:, 0], agc_s.at[kv])
        wait(compact[kv].at[0], cc_s.at[kv])
        wait(part.at[kv, pl.ds(0, 7)], rs_s.at[kv, 0])
        wait(direct.at[kv], rs_s.at[kv, 1])
        wait(relayed.at[kv], rs_s.at[kv, 2])


def hand_on(*refs):
    sem = refs[8]
    copies = [pltpu.make_async_copy(refs[i], refs[4 + i], sem.at[i]) for i in range(4)]
    for copy in copies:
        copy.start()
    for copy in copies:
        copy.wait()


def on_device(resp_q, resp_kv, prompt_kv, grad_out, lengths, resp_lists, owner_map):
    anywhere = pl.BlockSpec(memory_space=pl.ANY)
    in_vmem = pl.BlockSpec(memory_space=pltpu.VMEM)
    rows = resp_q.shape[0]
    dma = pltpu.SemaphoreType.DMA
    results = pl.pallas_call(
        kernel,
        name="attention",
        out_shape=(
            jax.ShapeDtypeStruct(resp_q.shape, BF),
            jax.ShapeDtypeStruct(resp_q.shape, BF),
            jax.ShapeDtypeStruct(resp_kv.shape, BF),
            jax.ShapeDtypeStruct(prompt_kv.shape, BF),
        ),
        in_specs=[anywhere] * 7,
        out_specs=(anywhere, anywhere, anywhere, in_vmem),
        scratch_shapes=[
            pltpu.VMEM((T, rows, HW), BF),
            pltpu.VMEM((T, rows, HW), BF),
            pltpu.VMEM((T, rows, KW), BF),
            pltpu.VMEM((T, rows, HW), BF),
            pltpu.VMEM((T, rows, HW), BF),
            pltpu.VMEM((T, rows, KW), BF),
            pltpu.VMEM((2, 2, Z, BR, HD), BF),
            pltpu.VMEM((2, 2, Z, BR, HD), BF),
            pltpu.VMEM((SLOTS, KEYS, HD), BF),
            pltpu.VMEM((SLOTS, KEYS, HD), BF),
            pltpu.VMEM((SLOTS, KEYS, GROUP * LR), F32),
            pltpu.VMEM((SLOTS, KEYS, GROUP * LR), BF),
            pltpu.VMEM((KEYS, GROUP * LR), BF),
            pltpu.VMEM((2, SLOTS, BLOCKS, BR, HD), BF),
            pltpu.VMEM((2, SLOTS, BLOCKS, BR, HD), BF),
            pltpu.VMEM((2, Z, 2, BR, HD), BF),
            pltpu.VMEM((2, len(DIRECT), BR, HD), BF),
            pltpu.VMEM((2, 4, 2, BR, HD), BF),
            pltpu.VMEM((2, 3, 2, BR, HD), BF),
            pltpu.VMEM((2, 4, BR, HD), BF),
            pltpu.SMEM(lengths.shape, jnp.int32),
            pltpu.SMEM(resp_lists.shape[::-1], jnp.int32),
            pltpu.SMEM(owner_map.shape, jnp.int32),
            dma((8,)),
            dma((3,)),
            dma((3,)),
            dma((2,)),
            dma((2, 7)),
            dma((2,)),
            dma((2,)),
            dma((2,)),
            dma((2,)),
            dma((3,)),
            dma((3,)),
            dma((2,)),
            dma((2,)),
            dma((2, 3)),
            dma((2, 4)),
        ],
        compiler_params=pltpu.CompilerParams(
            collective_id=0, has_side_effects=True, vmem_limit_bytes=60 * 1024 * 1024
        ),
    )(resp_q, resp_kv, prompt_kv, grad_out, lengths, resp_lists.T, owner_map)
    return pl.pallas_call(
        hand_on,
        name="hand_on",
        out_shape=tuple(jax.ShapeDtypeStruct(r.shape, r.dtype) for r in results),
        in_specs=[in_vmem] * 4,
        out_specs=(anywhere,) * 4,
        scratch_shapes=[dma((4,))],
    )(*results)


def solution(mesh):
    rows = P(("dp", "tensor"), None)
    return jax.shard_map(
        on_device,
        mesh=mesh,
        in_specs=(rows, rows, P("dp", "tensor"), rows, P(), P(), P()),
        out_specs=(rows, rows, rows, P("dp", "tensor")),
        check_vma=False,
    )
```

```python
import math

import jax
import jax.numpy as jnp
from jax import lax
from jax.experimental import pallas as pl
from jax.experimental.pallas import tpu as pltpu
from jax.sharding import PartitionSpec as P

MESH = pl.DeviceIdType.MESH
BF = jnp.bfloat16
F32 = jnp.float32
HD = 128
BLOCKS = 8
G = 16
Z = 16
T = 8
SLOTS = 2
LR = 64
GROUP = 8
BR = 32
PL = BLOCKS * BR
KEYS = PL + LR
HW = GROUP * HD
KW = 2 * HD
HALF = GROUP // 2
WIDE = HALF * LR
SCALE = 1.0 / math.sqrt(HD)
NEAR = (4, -4, 3, -3, 2, -2, 1, -1)
K, V = 0, 1


def dot(a, b, dims):
    return lax.dot_general(a, b, (dims, ((), ())), preferred_element_type=F32)


def kernel(
    q_in, kv_in, pkv_in, g_in, lengths_in, lists_in, owners_in,
    att_out, qg_out, rg_out, pg_out,
    qbuf, gbuf, kvbuf, obuf, dqbuf, rgbuf,
    table_k, table_v, kcat, vcat, probs_f, probs_t, dscore_t,
    compact_k, compact_v, part, direct, relay_a, relay_b, relayed, ypart, lengths, lists, owners,
    loc, a2a_s, a2a_r, agz_s, agz_r, agy_s, agy_r, agc_s, agc_r, back_s, back_r, cc_s, cc_r, rs_s, rs_r,
):
    table, compact = (table_k, table_v), (compact_k, compact_v)
    dp = lax.axis_index("dp")
    t = lax.axis_index("tensor")
    core = lax.rem(dp, 2)
    z = lax.rem(dp // 2, Z)
    y = dp // (2 * Z)

    way = 1 - 2 * core

    def at(a, d):
        return ((y + a - 2 * a * y) * (2 * Z) + lax.rem(z + way * d + Z, Z) * 2 + core, t)

    other_core = (y * (2 * Z) + z * 2 + (1 - core), t)
    peers = [lax.rem(t + k, T) for k in range(1, T)]

    def send(src, dst, s, r, device):
        pltpu.make_async_remote_copy(
            src_ref=src, dst_ref=dst, send_sem=s, recv_sem=r, device_id=device, device_id_type=MESH
        ).start()

    def wait(ref, sem):
        pltpu.make_async_copy(ref, ref, sem).wait()

    def columns(width, index):
        return pl.ds(pl.multiple_of(index * width, width), width)

    barrier = pltpu.get_barrier_semaphore()
    greeted = [(dp, p) for p in peers] + [at(a, d) for d in NEAR for a in (1, 0)] + [at(1, 0), other_core]
    for device in greeted:
        pl.semaphore_signal(barrier, inc=1, device_id=device, device_id_type=MESH)
    local = [
        pltpu.make_async_copy(pkv_in.at[:, :HD], table[K].at[0, 0, 8], loc.at[0]),
        pltpu.make_async_copy(pkv_in.at[:, HD:], table[V].at[0, 0, 8], loc.at[1]),
        pltpu.make_async_copy(kv_in.at[:, columns(KW, t)], kvbuf.at[t], loc.at[2]),
        pltpu.make_async_copy(q_in.at[:, columns(HW, t)], qbuf.at[t], loc.at[3]),
        pltpu.make_async_copy(g_in.at[:, columns(HW, t)], gbuf.at[t], loc.at[4]),
        pltpu.make_async_copy(lengths_in, lengths, loc.at[5]),
        pltpu.make_async_copy(lists_in, lists, loc.at[6]),
        pltpu.make_async_copy(owners_in, owners, loc.at[7]),
    ]
    for copy in local:
        copy.start()
    for copy in local[:2]:
        copy.wait()
    pl.semaphore_wait(barrier, len(greeted))

    def arrival(a, slot):
        return 0 if slot == 4 else 1 if slot == 12 else 2 if 4 < slot < 12 else 3 + 2 * a if slot < 4 else 4 + 2 * a

    def gather(kv, a, slot, d):
        to = slot - d
        send(table[kv].at[0, 0, slot], table[kv].at[a, 0, to], agz_s.at[kv], agz_r.at[kv, arrival(a, to)], at(a, d))

    def to_heads(a, src, dst, width):
        for p in peers:
            send(src.at[:, columns(width, p)], dst.at[t], a2a_s.at[a], a2a_r.at[a], (dp, p))

    for d in NEAR:
        gather(K, 0, 8, d)
    for d in NEAR:
        gather(V, 0, 8, d)
    to_heads(0, kv_in, kvbuf, KW)
    to_heads(1, q_in, qbuf, HW)
    to_heads(2, g_in, gbuf, HW)

    for kv in (K, V):
        wait(table[kv].at[0, 0, 4], agz_r.at[kv, 0])
        for d in (4, 3, 2, 1):
            for a in (1, 0):
                gather(kv, a, 4, d)
        wait(table[kv].at[0, 0, 12], agz_r.at[kv, 1])
        for d in (-3, -2, -1):
            for a in (1, 0):
                gather(kv, a, 12, d)

    groups = (pl.ds(4, 9), pl.ds(0, 4), pl.ds(13, 3))

    def over_core(kv, a, i):
        r = groups[i]
        send(table[kv].at[a, 0, r], table[kv].at[a, 1, r], agc_s.at[kv], agc_r.at[kv], other_core)

    for kv in (K, V):
        wait(table[kv].at[0, 0, pl.ds(4, 6)], agz_r.at[kv, 2])
        near = groups[0]
        send(table[kv].at[0, 0, near], table[kv].at[1, 0, near], agy_s.at[kv], agy_r.at[kv], at(1, 0))
        over_core(kv, 0, 0)

    for copy in local[5:]:
        copy.wait()
    resp = [lists[s, dp] for s in range(SLOTS)]
    prompt = [lax.div(a, G) for a in resp]
    length = [lengths[a] for a in resp]

    def find(j, found):
        code = owners[j]
        return tuple(
            jnp.where(code == prompt[s] * BLOCKS + b, j, found[s * BLOCKS + b])
            for s in range(SLOTS)
            for b in range(BLOCKS)
        )

    found = lax.fori_loop(0, 4 * Z, find, tuple(jnp.int32(0) for _ in range(SLOTS * BLOCKS)), unroll=4)

    def pick(cat, kv, s):
        for b in range(BLOCKS):
            j = found[s * BLOCKS + b]
            jy, jz, jc = lax.div(j, 2 * Z), lax.rem(lax.div(j, 2), Z), lax.rem(j, 2)
            slot = lax.rem((1 - 2 * jc) * (jz - z) + 8 + Z, Z)
            block = table[kv][jnp.where(jy == y, 0, 1), jnp.where(jc == core, 0, 1), slot]
            cat[s, b * BR : (b + 1) * BR] = block

    for kv in (K, V):
        wait(table[kv].at[1, 0, groups[0]], agy_r.at[kv])
        over_core(kv, 1, 0)
        for i in (1, 2):
            for a in range(2):
                wait(table[kv].at[a, 0, groups[i]], agz_r.at[kv, 2 + i + 2 * a])
                over_core(kv, a, i)
    for copy in local[2:5]:
        copy.wait()
    for a, buf in enumerate((kvbuf, qbuf, gbuf)):
        wait(buf.at[pl.ds(0, T - 1)], a2a_r.at[a])
    for s in range(SLOTS):
        row = lax.broadcasted_iota(jnp.int32, (LR, HW), 0)
        masked = jnp.where(row < length[s], gbuf[4 * s : 4 * s + 4].reshape(LR, HW).astype(F32), 0.0)
        gbuf[4 * s : 4 * s + 4] = masked.astype(BF).reshape(4, 16, HW)
        own = kvbuf[4 * s : 4 * s + 4].reshape(LR, KW)
        kcat[s, PL:] = own[:, :HD]
        vcat[s, PL:] = own[:, HD:]

    def stacked(buf, s, first, heads):
        cols = [buf[4 * s : 4 * s + 4, :, pl.ds(pl.multiple_of(first + h * HD, HD), HD)].reshape(LR, HD) for h in range(heads)]
        return jnp.concatenate(cols, axis=0)

    def hand_over(kv, s, grad):
        out = grad.astype(BF)
        compact[kv][0, s] = out[:PL].reshape(BLOCKS, BR, HD)
        rgbuf[4 * s : 4 * s + 4, :, kv * HD : (kv + 1) * HD] = out[PL:].reshape(4, 16, HD)
        send(compact[kv].at[0, s], compact[kv].at[1, s], cc_s.at[kv], cc_r.at[kv], other_core)

    wait(table[K].at[:, 1], agc_r.at[K])
    for s in range(SLOTS):
        pick(kcat, K, s)
        n, keys = length[s], kcat[s]

        def first_pass(h, _, s=s, n=n, keys=keys):
            q = stacked(qbuf, s, h * HALF * HD, HALF)
            scores = dot(keys, q, ((1,), (1,))) * SCALE
            u = lax.broadcasted_iota(jnp.int32, (LR, WIDE), 0)
            at = lax.rem(lax.broadcasted_iota(jnp.int32, (LR, WIDE), 1), LR)
            own_scores = jnp.where((u <= at) & (u < n), scores[PL:], -jnp.inf)
            scores = jnp.concatenate([scores[:PL], own_scores], axis=0)
            top = jnp.max(scores, axis=0, keepdims=True)
            e = jnp.exp(scores - top)
            probs = e * (1.0 / jnp.sum(e, axis=0, keepdims=True))
            cols = columns(WIDE, h)
            probs_f[s, :, cols] = probs
            probs_t[s, :, cols] = probs.astype(BF)
            return 0

        lax.fori_loop(0, 2, first_pass, 0, unroll=True)
        hand_over(V, s, dot(probs_t[s], stacked(gbuf, s, 0, GROUP), ((1,), (0,))))

    learner2 = dp + 1 - 2 * core
    slot_prompts = prompt + [lax.div(lists[s, learner2], G) for s in range(SLOTS)]

    def fill(kv, first, count):
        def one(i, _):
            k = lax.rem(first + i, Z)
            for a in range(2):
                code = owners[(y + a - 2 * a * y) * (2 * Z) + lax.rem(z + way * (k - 8) + Z, Z) * 2 + core]
                p, b = lax.div(code, BLOCKS), lax.rem(code, BLOCKS)
                total = jnp.zeros((BR, HD), F32)
                for c in range(2):
                    for s in range(SLOTS):
                        hit = slot_prompts[c * SLOTS + s] == p
                        total = total + jnp.where(hit, compact[kv][c, s, b].astype(F32), 0.0)
                part[kv, a, k] = total.astype(BF)
            return 0

        lax.fori_loop(0, count, one, 0)

    def far(kv):
        wait(compact[kv].at[1], cc_r.at[kv])
        fill(kv, 13, 4)
        for i, d in enumerate((4, 3, 2, 1)):
            send(part.at[kv, :, (8 + d + 4) % Z], relay_a.at[kv, i], rs_s.at[kv, 0], rs_r.at[kv, 0], at(0, d))
        fill(kv, 1, 3)
        for i, d in enumerate((-3, -2, -1)):
            send(part.at[kv, :, 8 + d - 4], relay_b.at[kv, i], rs_s.at[kv, 0], rs_r.at[kv, 1], at(0, d))

    near_slots = pl.ds(5, 7)

    def near_y(kv):
        fill(kv, 4, 9)
        send(part.at[kv, 1, near_slots], ypart.at[kv], rs_s.at[kv, 1], rs_r.at[kv, 2], at(1, 0))

    def near_z(kv):
        wait(ypart.at[kv], rs_r.at[kv, 2])
        part[kv, 0, near_slots] = (part[kv, 0, near_slots].astype(F32) + ypart[kv].astype(F32)).astype(BF)
        for i, d in enumerate(NEAR[2:]):
            send(part.at[kv, 0, 8 + d], direct.at[kv, i], rs_s.at[kv, 2], rs_r.at[kv, 3], at(0, d))

    def relay(kv):
        for j, (slot, buf, count) in enumerate(((12, relay_a, 4), (4, relay_b, 3))):
            wait(buf.at[kv], rs_r.at[kv, j])
            total = part[kv, :, slot].astype(F32)
            for i in range(count):
                total = total + buf[kv, i].astype(F32)
            part[kv, :, slot] = total.astype(BF)
            for a in (1, 0):
                send(part.at[kv, a, slot], relayed.at[kv, 2 * j + a], rs_s.at[kv, 3], rs_r.at[kv, 4], at(a, slot - 8))

    def finish(kv):
        wait(direct.at[kv], rs_r.at[kv, 3])
        total = part[kv, 0, 8].astype(F32)
        for i in range(6):
            total = total + direct[kv, i].astype(F32)
        wait(relayed.at[kv], rs_r.at[kv, 4])
        for i in range(4):
            total = total + relayed[kv, i].astype(F32)
        pg_out[:, kv * HD : (kv + 1) * HD] = total.astype(BF)

    wait(table[V].at[:, 1], agc_r.at[V])
    for s in range(SLOTS):
        pick(vcat, V, s)
        values = vcat[s]

        def second_pass(h, _, s=s, values=values):
            g = stacked(gbuf, s, h * HALF * HD, HALF)
            cols = columns(WIDE, h)
            dprob = dot(values, g, ((1,), (1,)))
            delta = jnp.sum(probs_t[s, :, cols].astype(F32) * dprob, axis=0, keepdims=True)
            dscore_t[s, :, cols] = (probs_f[s, :, cols] * (dprob - delta) * SCALE).astype(BF)
            return 0

        lax.fori_loop(0, 2, second_pass, 0, unroll=True)
        hand_over(K, s, dot(dscore_t[s], stacked(qbuf, s, 0, GROUP), ((1,), (0,))))
        if s == 0:
            far(V)

    results = ((obuf, att_out, HW), (dqbuf, qg_out, HW), (rgbuf, rg_out, KW))

    def to_rows(a):
        src, to, width = results[a]
        for p in peers:
            send(src.at[p], to.at[:, columns(width, t)], back_s.at[a], back_r.at[a], (dp, p))
        copy = pltpu.make_async_copy(src.at[t], to.at[:, columns(width, t)], loc.at[a])
        copy.start()
        return copy

    def back(a, left, right):
        for s in range(SLOTS):
            for h in range(2):
                rows = dot(left[s, :, h * WIDE : (h + 1) * WIDE], right[s], ((0,), (0,)))
                for i in range(HALF):
                    head = slice((h * HALF + i) * HD, (h * HALF + i + 1) * HD)
                    values = rows[i * LR : (i + 1) * LR]
                    if a == 0:
                        live = lax.broadcasted_iota(jnp.int32, (LR, HD), 0) < length[s]
                        values = jnp.where(live, values, 0.0)
                    results[a][0][4 * s : 4 * s + 4, :, head] = values.astype(BF).reshape(4, 16, HD)

    far(K)
    near_y(V)
    near_y(K)
    back(0, probs_t, vcat)
    near_z(V)
    near_z(K)
    stay = [to_rows(0)]
    relay(V)
    back(1, dscore_t, kcat)
    relay(K)
    stay.append(to_rows(2))
    stay.append(to_rows(1))
    finish(V)
    finish(K)

    for a, (buf, _, _) in enumerate(results):
        wait(buf.at[pl.ds(0, T - 1)], back_r.at[a])
        wait(buf.at[pl.ds(0, T - 1)], back_s.at[a])
    for copy in stay:
        copy.wait()
    for a, buf in enumerate((kvbuf, qbuf, gbuf)):
        wait(buf.at[pl.ds(0, T - 1)], a2a_s.at[a])
    for kv in (K, V):
        wait(table[kv].at[:, 0, pl.ds(0, 11)], agz_s.at[kv])
        wait(table[kv].at[0, 0, near], agy_s.at[kv])
        wait(table[kv].at[:, 0], agc_s.at[kv])
        wait(compact[kv].at[0], cc_s.at[kv])
        wait(part.at[kv, :, pl.ds(0, 7)], rs_s.at[kv, 0])
        wait(ypart.at[kv], rs_s.at[kv, 1])
        wait(direct.at[kv], rs_s.at[kv, 2])
        wait(relayed.at[kv], rs_s.at[kv, 3])


def hand_on(*refs):
    held, sem = refs[8:12], refs[12]
    copies = [
        (pltpu.make_async_copy(refs[i], held[i], sem.at[i]), pltpu.make_async_copy(held[i], refs[4 + i], sem.at[i]))
        for i in range(4)
    ]
    for first, _ in copies:
        first.start()
    for first, second in copies:
        first.wait()
        second.start()
    for _, second in copies:
        second.wait()


def on_device(resp_q, resp_kv, prompt_kv, grad_out, lengths, resp_lists, owner_map):
    anywhere = pl.BlockSpec(memory_space=pl.ANY)
    in_vmem = pl.BlockSpec(memory_space=pltpu.VMEM)
    rows = resp_q.shape[0]
    dma = pltpu.SemaphoreType.DMA
    results = pl.pallas_call(
        kernel,
        name="attention",
        out_shape=(
            jax.ShapeDtypeStruct(resp_q.shape, BF),
            jax.ShapeDtypeStruct(resp_q.shape, BF),
            jax.ShapeDtypeStruct(resp_kv.shape, BF),
            jax.ShapeDtypeStruct(prompt_kv.shape, BF),
        ),
        in_specs=[anywhere] * 7,
        out_specs=(anywhere, anywhere, anywhere, in_vmem),
        scratch_shapes=[
            pltpu.VMEM((T, rows, HW), BF),
            pltpu.VMEM((T, rows, HW), BF),
            pltpu.VMEM((T, rows, KW), BF),
            pltpu.VMEM((T, rows, HW), BF),
            pltpu.VMEM((T, rows, HW), BF),
            pltpu.VMEM((T, rows, KW), BF),
            pltpu.VMEM((2, 2, Z, BR, HD), BF),
            pltpu.VMEM((2, 2, Z, BR, HD), BF),
            pltpu.VMEM((SLOTS, KEYS, HD), BF),
            pltpu.VMEM((SLOTS, KEYS, HD), BF),
            pltpu.VMEM((SLOTS, KEYS, GROUP * LR), F32),
            pltpu.VMEM((SLOTS, KEYS, GROUP * LR), BF),
            pltpu.VMEM((SLOTS, KEYS, GROUP * LR), BF),
            pltpu.VMEM((2, SLOTS, BLOCKS, BR, HD), BF),
            pltpu.VMEM((2, SLOTS, BLOCKS, BR, HD), BF),
            pltpu.VMEM((2, 2, Z, BR, HD), BF),
            pltpu.VMEM((2, 6, BR, HD), BF),
            pltpu.VMEM((2, 4, 2, BR, HD), BF),
            pltpu.VMEM((2, 3, 2, BR, HD), BF),
            pltpu.VMEM((2, 4, BR, HD), BF),
            pltpu.VMEM((2, 7, BR, HD), BF),
            pltpu.SMEM(lengths.shape, jnp.int32),
            pltpu.SMEM(resp_lists.shape[::-1], jnp.int32),
            pltpu.SMEM(owner_map.shape, jnp.int32),
            dma((8,)),
            dma((3,)),
            dma((3,)),
            dma((2,)),
            dma((2, 7)),
            dma((2,)),
            dma((2,)),
            dma((2,)),
            dma((2,)),
            dma((3,)),
            dma((3,)),
            dma((2,)),
            dma((2,)),
            dma((2, 4)),
            dma((2, 5)),
        ],
        compiler_params=pltpu.CompilerParams(
            collective_id=0, has_side_effects=True, vmem_limit_bytes=60 * 1024 * 1024
        ),
    )(resp_q, resp_kv, prompt_kv, grad_out, lengths, resp_lists.T, owner_map)
    return pl.pallas_call(
        hand_on,
        name="hand_on",
        out_shape=tuple(jax.ShapeDtypeStruct(r.shape, r.dtype) for r in results),
        in_specs=[anywhere] * 4,
        out_specs=(anywhere,) * 4,
        scratch_shapes=[pltpu.VMEM(r.shape, r.dtype) for r in results] + [dma((4,))],
        compiler_params=pltpu.CompilerParams(vmem_limit_bytes=60 * 1024 * 1024),
    )(*results)


def solution(mesh):
    rows = P(("dp", "tensor"), None)
    return jax.shard_map(
        on_device,
        mesh=mesh,
        in_specs=(rows, rows, P("dp", "tensor"), rows, P(), P(), P()),
        out_specs=(rows, rows, rows, P("dp", "tensor")),
        check_vma=False,
    )
```

```python
import math

import jax
import jax.numpy as jnp
from jax import lax
from jax.experimental import pallas as pl
from jax.experimental.pallas import tpu as pltpu
from jax.sharding import PartitionSpec as P

MESH = pl.DeviceIdType.MESH
BF = jnp.bfloat16
F32 = jnp.float32
HD = 128
BLOCKS = 8
G = 16
Z = 16
T = 8
SLOTS = 2
LR = 64
GROUP = 8
BR = 32
PL = BLOCKS * BR
KEYS = PL + LR
HW = GROUP * HD
KW = 2 * HD
HALF = GROUP // 2
WIDE = HALF * LR
SCALE = 1.0 / math.sqrt(HD)
NEAR = (4, -4, 3, -3, 2, -2, 1, -1)
K, V = 0, 1


def dot(a, b, dims):
    return lax.dot_general(a, b, (dims, ((), ())), preferred_element_type=F32)


def kernel(
    q_in, kv_in, pkv_in, g_in, lengths_in, lists_in, owners_in,
    att_out, qg_out, rg_out, pg_out,
    qbuf, gbuf, kvbuf, obuf, dqbuf, rgbuf,
    table_k, table_v, kcat, vcat, probs_f, probs_t, dscore_t,
    compact_k, compact_v, part, direct, relay_a, relay_b, relayed, ypart, lengths, lists, owners,
    loc, a2a_s, a2a_r, agz_s, agz_r, agy_s, agy_r, agc_s, agc_r, back_s, back_r, cc_s, cc_r, rs_s, rs_r, heard,
):
    table, compact = (table_k, table_v), (compact_k, compact_v)
    dp = lax.axis_index("dp")
    t = lax.axis_index("tensor")
    core = lax.rem(dp, 2)
    z = lax.rem(dp // 2, Z)
    y = dp // (2 * Z)

    way = 1 - 2 * core

    def at(a, d):
        return ((y + a - 2 * a * y) * (2 * Z) + lax.rem(z + way * d + Z, Z) * 2 + core, t)

    other_core = (y * (2 * Z) + z * 2 + (1 - core), t)
    peers = [lax.rem(t + k, T) for k in range(1, T)]

    def send(src, dst, s, r, device):
        pltpu.make_async_remote_copy(
            src_ref=src, dst_ref=dst, send_sem=s, recv_sem=r, device_id=device, device_id_type=MESH
        ).start()

    def wait(ref, sem):
        pltpu.make_async_copy(ref, ref, sem).wait()

    def columns(width, index):
        return pl.ds(pl.multiple_of(index * width, width), width)

    barrier = pltpu.get_barrier_semaphore()
    greeted = [(dp, p) for p in peers] + [at(0, d) for d in NEAR] + [at(1, 0), other_core]
    for device in greeted:
        pl.semaphore_signal(barrier, inc=1, device_id=device, device_id_type=MESH)
    local = [
        pltpu.make_async_copy(pkv_in.at[:, :HD], table[K].at[0, 0, 8], loc.at[0]),
        pltpu.make_async_copy(pkv_in.at[:, HD:], table[V].at[0, 0, 8], loc.at[1]),
        pltpu.make_async_copy(kv_in.at[:, columns(KW, t)], kvbuf.at[t], loc.at[2]),
        pltpu.make_async_copy(q_in.at[:, columns(HW, t)], qbuf.at[t], loc.at[3]),
        pltpu.make_async_copy(g_in.at[:, columns(HW, t)], gbuf.at[t], loc.at[4]),
        pltpu.make_async_copy(lengths_in, lengths, loc.at[5]),
        pltpu.make_async_copy(lists_in, lists, loc.at[6]),
        pltpu.make_async_copy(owners_in, owners, loc.at[7]),
    ]
    for copy in local:
        copy.start()
    for copy in local[:2]:
        copy.wait()
    pl.semaphore_wait(barrier, len(greeted))
    pl.semaphore_signal(heard, inc=1, device_id=at(1, 0), device_id_type=MESH)

    def arrival(a, slot):
        return 0 if slot == 4 else 1 if slot == 12 else 2 if 4 < slot < 12 else 3 + 2 * a if slot < 4 else 4 + 2 * a

    def gather(kv, a, slot, d):
        to = slot - d
        send(table[kv].at[0, 0, slot], table[kv].at[a, 0, to], agz_s.at[kv], agz_r.at[kv, arrival(a, to)], at(a, d))

    def to_heads(a, src, dst, width):
        for p in peers:
            send(src.at[:, columns(width, p)], dst.at[t], a2a_s.at[a], a2a_r.at[a], (dp, p))

    for d in NEAR:
        gather(K, 0, 8, d)
    for d in NEAR:
        gather(V, 0, 8, d)
    to_heads(0, kv_in, kvbuf, KW)
    to_heads(1, q_in, qbuf, HW)
    to_heads(2, g_in, gbuf, HW)

    pl.semaphore_wait(heard, 1)
    for kv in (K, V):
        wait(table[kv].at[0, 0, 4], agz_r.at[kv, 0])
        for d in (4, 3, 2, 1):
            for a in (1, 0):
                gather(kv, a, 4, d)
        wait(table[kv].at[0, 0, 12], agz_r.at[kv, 1])
        for d in (-3, -2, -1):
            for a in (1, 0):
                gather(kv, a, 12, d)

    groups = (pl.ds(4, 9), pl.ds(0, 4), pl.ds(13, 3))

    def over_core(kv, a, i):
        r = groups[i]
        send(table[kv].at[a, 0, r], table[kv].at[a, 1, r], agc_s.at[kv], agc_r.at[kv], other_core)

    for kv in (K, V):
        wait(table[kv].at[0, 0, pl.ds(4, 6)], agz_r.at[kv, 2])
        near = groups[0]
        send(table[kv].at[0, 0, near], table[kv].at[1, 0, near], agy_s.at[kv], agy_r.at[kv], at(1, 0))
        over_core(kv, 0, 0)

    for copy in local[5:]:
        copy.wait()
    resp = [lists[s, dp] for s in range(SLOTS)]
    prompt = [lax.div(a, G) for a in resp]
    length = [lengths[a] for a in resp]

    def find(j, found):
        code = owners[j]
        return tuple(
            jnp.where(code == prompt[s] * BLOCKS + b, j, found[s * BLOCKS + b])
            for s in range(SLOTS)
            for b in range(BLOCKS)
        )

    found = lax.fori_loop(0, 4 * Z, find, tuple(jnp.int32(0) for _ in range(SLOTS * BLOCKS)), unroll=4)

    def pick(cat, kv, s):
        for b in range(BLOCKS):
            j = found[s * BLOCKS + b]
            jy, jz, jc = lax.div(j, 2 * Z), lax.rem(lax.div(j, 2), Z), lax.rem(j, 2)
            slot = lax.rem((1 - 2 * jc) * (jz - z) + 8 + Z, Z)
            block = table[kv][jnp.where(jy == y, 0, 1), jnp.where(jc == core, 0, 1), slot]
            cat[s, b * BR : (b + 1) * BR] = block

    for kv in (K, V):
        wait(table[kv].at[1, 0, groups[0]], agy_r.at[kv])
        over_core(kv, 1, 0)
        for i in (1, 2):
            for a in range(2):
                wait(table[kv].at[a, 0, groups[i]], agz_r.at[kv, 2 + i + 2 * a])
                over_core(kv, a, i)
    for copy in local[2:5]:
        copy.wait()
    for a, buf in enumerate((kvbuf, qbuf, gbuf)):
        wait(buf.at[pl.ds(0, T - 1)], a2a_r.at[a])
    for s in range(SLOTS):
        row = lax.broadcasted_iota(jnp.int32, (LR, HW), 0)
        masked = jnp.where(row < length[s], gbuf[4 * s : 4 * s + 4].reshape(LR, HW).astype(F32), 0.0)
        gbuf[4 * s : 4 * s + 4] = masked.astype(BF).reshape(4, 16, HW)
        own = kvbuf[4 * s : 4 * s + 4].reshape(LR, KW)
        kcat[s, PL:] = own[:, :HD]
        vcat[s, PL:] = own[:, HD:]

    def stacked(buf, s, first, heads):
        cols = [buf[4 * s : 4 * s + 4, :, pl.ds(pl.multiple_of(first + h * HD, HD), HD)].reshape(LR, HD) for h in range(heads)]
        return jnp.concatenate(cols, axis=0)

    def hand_over(kv, s, grad):
        out = grad.astype(BF)
        compact[kv][0, s] = out[:PL].reshape(BLOCKS, BR, HD)
        rgbuf[4 * s : 4 * s + 4, :, kv * HD : (kv + 1) * HD] = out[PL:].reshape(4, 16, HD)
        send(compact[kv].at[0, s], compact[kv].at[1, s], cc_s.at[kv], cc_r.at[kv], other_core)

    wait(table[K].at[:, 1], agc_r.at[K])
    for s in range(SLOTS):
        pick(kcat, K, s)
        n, keys = length[s], kcat[s]

        def first_pass(h, _, s=s, n=n, keys=keys):
            q = stacked(qbuf, s, h * HALF * HD, HALF)
            scores = dot(keys, q, ((1,), (1,))) * SCALE
            u = lax.broadcasted_iota(jnp.int32, (LR, WIDE), 0)
            at = lax.rem(lax.broadcasted_iota(jnp.int32, (LR, WIDE), 1), LR)
            own_scores = jnp.where((u <= at) & (u < n), scores[PL:], -jnp.inf)
            scores = jnp.concatenate([scores[:PL], own_scores], axis=0)
            top = jnp.max(scores, axis=0, keepdims=True)
            e = jnp.exp(scores - top)
            probs = e * (1.0 / jnp.sum(e, axis=0, keepdims=True))
            cols = columns(WIDE, h)
            probs_f[s, :, cols] = probs
            probs_t[s, :, cols] = probs.astype(BF)
            return 0

        lax.fori_loop(0, 2, first_pass, 0, unroll=True)
        hand_over(V, s, dot(probs_t[s], stacked(gbuf, s, 0, GROUP), ((1,), (0,))))

    learner2 = dp + 1 - 2 * core
    slot_prompts = prompt + [lax.div(lists[s, learner2], G) for s in range(SLOTS)]

    def fill(kv, first, count):
        def one(i, _):
            k = lax.rem(first + i, Z)
            for a in range(2):
                code = owners[(y + a - 2 * a * y) * (2 * Z) + lax.rem(z + way * (k - 8) + Z, Z) * 2 + core]
                p, b = lax.div(code, BLOCKS), lax.rem(code, BLOCKS)
                total = jnp.zeros((BR, HD), F32)
                for c in range(2):
                    for s in range(SLOTS):
                        hit = slot_prompts[c * SLOTS + s] == p
                        total = total + jnp.where(hit, compact[kv][c, s, b].astype(F32), 0.0)
                part[kv, a, k] = total.astype(BF)
            return 0

        if count == 1:
            one(0, 0)
        else:
            lax.fori_loop(0, count, one, 0)

    def far(kv):
        wait(compact[kv].at[1], cc_r.at[kv])
        for i, d in enumerate((4, 3, 2, 1)):
            fill(kv, (8 + d + 4) % Z, 1)
            send(part.at[kv, :, (8 + d + 4) % Z], relay_a.at[kv, i], rs_s.at[kv, 0], rs_r.at[kv, 0], at(0, d))
        for i, d in enumerate((-3, -2, -1)):
            fill(kv, 8 + d - 4, 1)
            send(part.at[kv, :, 8 + d - 4], relay_b.at[kv, i], rs_s.at[kv, 0], rs_r.at[kv, 1], at(0, d))

    near_slots = pl.ds(5, 7)

    def near_y(kv):
        fill(kv, 4, 9)
        send(part.at[kv, 1, near_slots], ypart.at[kv], rs_s.at[kv, 1], rs_r.at[kv, 2], at(1, 0))

    def near_z(kv):
        wait(ypart.at[kv], rs_r.at[kv, 2])
        part[kv, 0, near_slots] = (part[kv, 0, near_slots].astype(F32) + ypart[kv].astype(F32)).astype(BF)
        for i, d in enumerate(NEAR[2:]):
            send(part.at[kv, 0, 8 + d], direct.at[kv, i], rs_s.at[kv, 2], rs_r.at[kv, 3], at(0, d))

    def relay(kv):
        for j, (slot, buf, count) in enumerate(((12, relay_a, 4), (4, relay_b, 3))):
            wait(buf.at[kv], rs_r.at[kv, j])
            total = part[kv, :, slot].astype(F32)
            for i in range(count):
                total = total + buf[kv, i].astype(F32)
            part[kv, :, slot] = total.astype(BF)
            for a in (1, 0):
                send(part.at[kv, a, slot], relayed.at[kv, 2 * j + a], rs_s.at[kv, 3], rs_r.at[kv, 4], at(a, slot - 8))

    def finish(kv):
        wait(direct.at[kv], rs_r.at[kv, 3])
        total = part[kv, 0, 8].astype(F32)
        for i in range(6):
            total = total + direct[kv, i].astype(F32)
        wait(relayed.at[kv], rs_r.at[kv, 4])
        for i in range(4):
            total = total + relayed[kv, i].astype(F32)
        pg_out[:, kv * HD : (kv + 1) * HD] = total.astype(BF)

    wait(table[V].at[:, 1], agc_r.at[V])
    for s in range(SLOTS):
        pick(vcat, V, s)
        values = vcat[s]

        def second_pass(h, _, s=s, values=values):
            g = stacked(gbuf, s, h * HALF * HD, HALF)
            cols = columns(WIDE, h)
            dprob = dot(values, g, ((1,), (1,)))
            delta = jnp.sum(probs_t[s, :, cols].astype(F32) * dprob, axis=0, keepdims=True)
            dscore_t[s, :, cols] = (probs_f[s, :, cols] * (dprob - delta) * SCALE).astype(BF)
            return 0

        lax.fori_loop(0, 2, second_pass, 0, unroll=True)
        hand_over(K, s, dot(dscore_t[s], stacked(qbuf, s, 0, GROUP), ((1,), (0,))))
        if s == 0:
            far(V)

    results = ((obuf, att_out, HW), (dqbuf, qg_out, HW), (rgbuf, rg_out, KW))

    def to_rows(a):
        src, to, width = results[a]
        for p in peers:
            send(src.at[p], to.at[:, columns(width, t)], back_s.at[a], back_r.at[a], (dp, p))
        copy = pltpu.make_async_copy(src.at[t], to.at[:, columns(width, t)], loc.at[a])
        copy.start()
        return copy

    def back(a, left, right):
        for s in range(SLOTS):
            for h in range(2):
                rows = dot(left[s, :, h * WIDE : (h + 1) * WIDE], right[s], ((0,), (0,)))
                for i in range(HALF):
                    head = slice((h * HALF + i) * HD, (h * HALF + i + 1) * HD)
                    values = rows[i * LR : (i + 1) * LR]
                    if a == 0:
                        live = lax.broadcasted_iota(jnp.int32, (LR, HD), 0) < length[s]
                        values = jnp.where(live, values, 0.0)
                    results[a][0][4 * s : 4 * s + 4, :, head] = values.astype(BF).reshape(4, 16, HD)

    far(K)
    near_y(V)
    near_y(K)
    back(0, probs_t, vcat)
    near_z(V)
    near_z(K)
    stay = [to_rows(0)]
    relay(V)
    back(1, dscore_t, kcat)
    relay(K)
    stay.append(to_rows(2))
    stay.append(to_rows(1))
    finish(V)
    finish(K)

    for a, (buf, _, _) in enumerate(results):
        wait(buf.at[pl.ds(0, T - 1)], back_r.at[a])
        wait(buf.at[pl.ds(0, T - 1)], back_s.at[a])
    for copy in stay:
        copy.wait()
    for a, buf in enumerate((kvbuf, qbuf, gbuf)):
        wait(buf.at[pl.ds(0, T - 1)], a2a_s.at[a])
    for kv in (K, V):
        wait(table[kv].at[:, 0, pl.ds(0, 11)], agz_s.at[kv])
        wait(table[kv].at[0, 0, near], agy_s.at[kv])
        wait(table[kv].at[:, 0], agc_s.at[kv])
        wait(compact[kv].at[0], cc_s.at[kv])
        wait(part.at[kv, :, pl.ds(0, 7)], rs_s.at[kv, 0])
        wait(ypart.at[kv], rs_s.at[kv, 1])
        wait(direct.at[kv], rs_s.at[kv, 2])
        wait(relayed.at[kv], rs_s.at[kv, 3])


def hand_on(*refs):
    copies = [pltpu.make_async_copy(refs[i], refs[4 + i], refs[8].at[i]) for i in range(4)]
    for copy in copies:
        copy.start()
    for copy in copies:
        copy.wait()


def on_device(resp_q, resp_kv, prompt_kv, grad_out, lengths, resp_lists, owner_map):
    anywhere = pl.BlockSpec(memory_space=pl.ANY)
    in_vmem = pl.BlockSpec(memory_space=pltpu.VMEM)
    rows = resp_q.shape[0]
    dma = pltpu.SemaphoreType.DMA
    results = pl.pallas_call(
        kernel,
        name="attention",
        out_shape=(
            pltpu.VMEM(resp_q.shape, BF),
            pltpu.VMEM(resp_q.shape, BF),
            pltpu.VMEM(resp_kv.shape, BF),
            pltpu.VMEM(prompt_kv.shape, BF),
        ),
        in_specs=[anywhere] * 7,
        out_specs=(in_vmem,) * 4,
        scratch_shapes=[
            pltpu.VMEM((T, rows, HW), BF),
            pltpu.VMEM((T, rows, HW), BF),
            pltpu.VMEM((T, rows, KW), BF),
            pltpu.VMEM((T, rows, HW), BF),
            pltpu.VMEM((T, rows, HW), BF),
            pltpu.VMEM((T, rows, KW), BF),
            pltpu.VMEM((2, 2, Z, BR, HD), BF),
            pltpu.VMEM((2, 2, Z, BR, HD), BF),
            pltpu.VMEM((SLOTS, KEYS, HD), BF),
            pltpu.VMEM((SLOTS, KEYS, HD), BF),
            pltpu.VMEM((SLOTS, KEYS, GROUP * LR), F32),
            pltpu.VMEM((SLOTS, KEYS, GROUP * LR), BF),
            pltpu.VMEM((SLOTS, KEYS, GROUP * LR), BF),
            pltpu.VMEM((2, SLOTS, BLOCKS, BR, HD), BF),
            pltpu.VMEM((2, SLOTS, BLOCKS, BR, HD), BF),
            pltpu.VMEM((2, 2, Z, BR, HD), BF),
            pltpu.VMEM((2, 6, BR, HD), BF),
            pltpu.VMEM((2, 4, 2, BR, HD), BF),
            pltpu.VMEM((2, 3, 2, BR, HD), BF),
            pltpu.VMEM((2, 4, BR, HD), BF),
            pltpu.VMEM((2, 7, BR, HD), BF),
            pltpu.SMEM(lengths.shape, jnp.int32),
            pltpu.SMEM(resp_lists.shape[::-1], jnp.int32),
            pltpu.SMEM(owner_map.shape, jnp.int32),
            dma((8,)),
            dma((3,)),
            dma((3,)),
            dma((2,)),
            dma((2, 7)),
            dma((2,)),
            dma((2,)),
            dma((2,)),
            dma((2,)),
            dma((3,)),
            dma((3,)),
            dma((2,)),
            dma((2,)),
            dma((2, 4)),
            dma((2, 5)),
            pltpu.SemaphoreType.REGULAR,
        ],
        compiler_params=pltpu.CompilerParams(
            collective_id=0, has_side_effects=True, vmem_limit_bytes=60 * 1024 * 1024
        ),
    )(resp_q, resp_kv, prompt_kv, grad_out, lengths, resp_lists.T, owner_map)
    return pl.pallas_call(
        hand_on,
        name="hand_on",
        out_shape=tuple(jax.ShapeDtypeStruct(r.shape, r.dtype) for r in results),
        in_specs=[in_vmem] * 4,
        out_specs=(anywhere,) * 4,
        scratch_shapes=[dma((4,))],
    )(*[pltpu.with_memory_space_constraint(r, pltpu.VMEM) for r in results])


def solution(mesh):
    rows = P(("dp", "tensor"), None)
    return jax.shard_map(
        on_device,
        mesh=mesh,
        in_specs=(rows, rows, P("dp", "tensor"), rows, P(), P(), P()),
        out_specs=(rows, rows, rows, P("dp", "tensor")),
        check_vma=False,
    )
```

```python
import math

import jax
import jax.numpy as jnp
from jax import lax
from jax.experimental import pallas as pl
from jax.experimental.pallas import tpu as pltpu
from jax.sharding import PartitionSpec as P

MESH = pl.DeviceIdType.MESH
BF = jnp.bfloat16
F32 = jnp.float32
HD = 128
BLOCKS = 8
G = 16
Z = 16
T = 8
SLOTS = 2
LR = 64
GROUP = 8
BR = 32
PL = BLOCKS * BR
KEYS = PL + LR
HW = GROUP * HD
KW = 2 * HD
HALF = GROUP // 2
WIDE = HALF * LR
SCALE = 1.0 / math.sqrt(HD)
NEAR = (4, -4, 3, -3, 2, -2, 1, -1)
K, V = 0, 1


def dot(a, b, dims):
    return lax.dot_general(a, b, (dims, ((), ())), preferred_element_type=F32)


def kernel(
    q_in, kv_in, pkv_in, g_in, lengths_in, lists_in, owners_in,
    att_out, qg_out, rg_out, pg_out,
    qbuf, gbuf, kvbuf, obuf, dqbuf, rgbuf,
    table_k, table_v, kcat, vcat, probs_f, probs_t, dscore_t,
    compact_k, compact_v, part, direct, relay_a, relay_b, relayed, ypart, lengths, lists, owners,
    loc, a2a_s, a2a_r, agz_s, agz_r, agy_s, agy_r, agc_s, agc_r, back_s, back_r, cc_s, cc_r, rs_s, rs_r, heard,
):
    table, compact = (table_k, table_v), (compact_k, compact_v)
    dp = lax.axis_index("dp")
    t = lax.axis_index("tensor")
    core = lax.rem(dp, 2)
    z = lax.rem(dp // 2, Z)
    y = dp // (2 * Z)

    way = 1 - 2 * core

    def at(a, d):
        return ((y + a - 2 * a * y) * (2 * Z) + lax.rem(z + way * d + Z, Z) * 2 + core, t)

    other_core = (y * (2 * Z) + z * 2 + (1 - core), t)
    hops = ((2, 1), (1, 1), (3, 1), (0, 1), (2, 0), (1, 0), (3, 0))
    peers = [lax.rem(t // 2 + dx, 4) * 2 + lax.rem(t + dy, 2) for dx, dy in hops]

    def send(src, dst, s, r, device):
        pltpu.make_async_remote_copy(
            src_ref=src, dst_ref=dst, send_sem=s, recv_sem=r, device_id=device, device_id_type=MESH
        ).start()

    def wait(ref, sem):
        pltpu.make_async_copy(ref, ref, sem).wait()

    def columns(width, index):
        return pl.ds(pl.multiple_of(index * width, width), width)

    barrier = pltpu.get_barrier_semaphore()
    greeted = [(dp, p) for p in peers] + [at(0, d) for d in NEAR] + [at(1, 0), other_core]
    for device in greeted:
        pl.semaphore_signal(barrier, inc=1, device_id=device, device_id_type=MESH)
    local = [
        pltpu.make_async_copy(pkv_in.at[:, :HD], table[K].at[0, 0, 8], loc.at[0]),
        pltpu.make_async_copy(pkv_in.at[:, HD:], table[V].at[0, 0, 8], loc.at[1]),
        pltpu.make_async_copy(kv_in.at[:, columns(KW, t)], kvbuf.at[t], loc.at[2]),
        pltpu.make_async_copy(q_in.at[:, columns(HW, t)], qbuf.at[t], loc.at[3]),
        pltpu.make_async_copy(g_in.at[:, columns(HW, t)], gbuf.at[t], loc.at[4]),
        pltpu.make_async_copy(lengths_in, lengths, loc.at[5]),
        pltpu.make_async_copy(lists_in, lists, loc.at[6]),
        pltpu.make_async_copy(owners_in, owners, loc.at[7]),
    ]
    for copy in local:
        copy.start()
    for copy in local[:2]:
        copy.wait()
    pl.semaphore_wait(barrier, len(greeted))
    pl.semaphore_signal(heard, inc=1, device_id=at(1, 0), device_id_type=MESH)

    def arrival(a, slot):
        return 0 if slot == 4 else 1 if slot == 12 else 2 if 4 < slot < 12 else 3 + 2 * a if slot < 4 else 4 + 2 * a

    def gather(kv, a, slot, d):
        to = slot - d
        send(table[kv].at[0, 0, slot], table[kv].at[a, 0, to], agz_s.at[kv], agz_r.at[kv, arrival(a, to)], at(a, d))

    def to_heads(a, src, dst, width):
        for p in peers:
            send(src.at[:, columns(width, p)], dst.at[t], a2a_s.at[a], a2a_r.at[a], (dp, p))

    for d in NEAR:
        gather(K, 0, 8, d)
    for d in NEAR:
        gather(V, 0, 8, d)
    to_heads(0, kv_in, kvbuf, KW)
    to_heads(1, q_in, qbuf, HW)
    to_heads(2, g_in, gbuf, HW)

    pl.semaphore_wait(heard, 1)
    for kv in (K, V):
        wait(table[kv].at[0, 0, 4], agz_r.at[kv, 0])
        for d in (4, 3, 2, 1):
            for a in (1, 0):
                gather(kv, a, 4, d)
        wait(table[kv].at[0, 0, 12], agz_r.at[kv, 1])
        for d in (-3, -2, -1):
            for a in (1, 0):
                gather(kv, a, 12, d)

    groups = (pl.ds(4, 9), pl.ds(0, 4), pl.ds(13, 3))

    def over_core(kv, a, i):
        r = groups[i]
        send(table[kv].at[a, 0, r], table[kv].at[a, 1, r], agc_s.at[kv], agc_r.at[kv], other_core)

    for kv in (K, V):
        wait(table[kv].at[0, 0, pl.ds(4, 6)], agz_r.at[kv, 2])
        near = groups[0]
        send(table[kv].at[0, 0, near], table[kv].at[1, 0, near], agy_s.at[kv], agy_r.at[kv], at(1, 0))
        over_core(kv, 0, 0)

    for copy in local[5:]:
        copy.wait()
    resp = [lists[s, dp] for s in range(SLOTS)]
    prompt = [lax.div(a, G) for a in resp]
    length = [lengths[a] for a in resp]

    def find(j, found):
        code = owners[j]
        return tuple(
            jnp.where(code == prompt[s] * BLOCKS + b, j, found[s * BLOCKS + b])
            for s in range(SLOTS)
            for b in range(BLOCKS)
        )

    found = lax.fori_loop(0, 4 * Z, find, tuple(jnp.int32(0) for _ in range(SLOTS * BLOCKS)), unroll=16)

    def pick(cat, kv, s):
        for b in range(BLOCKS):
            j = found[s * BLOCKS + b]
            jy, jz, jc = lax.div(j, 2 * Z), lax.rem(lax.div(j, 2), Z), lax.rem(j, 2)
            slot = lax.rem((1 - 2 * jc) * (jz - z) + 8 + Z, Z)
            block = table[kv][jnp.where(jy == y, 0, 1), jnp.where(jc == core, 0, 1), slot]
            cat[s, b * BR : (b + 1) * BR] = block

    for kv in (K, V):
        wait(table[kv].at[1, 0, groups[0]], agy_r.at[kv])
        over_core(kv, 1, 0)
        for i in (1, 2):
            for a in range(2):
                wait(table[kv].at[a, 0, groups[i]], agz_r.at[kv, 2 + i + 2 * a])
                over_core(kv, a, i)
    for copy in local[2:5]:
        copy.wait()
    for a, buf in enumerate((kvbuf, qbuf, gbuf)):
        wait(buf.at[pl.ds(0, T - 1)], a2a_r.at[a])
    for s in range(SLOTS):
        row = lax.broadcasted_iota(jnp.int32, (LR, HW), 0)
        masked = jnp.where(row < length[s], gbuf[4 * s : 4 * s + 4].reshape(LR, HW).astype(F32), 0.0)
        gbuf[4 * s : 4 * s + 4] = masked.astype(BF).reshape(4, 16, HW)
        own = kvbuf[4 * s : 4 * s + 4].reshape(LR, KW)
        kcat[s, PL:] = own[:, :HD]
        vcat[s, PL:] = own[:, HD:]

    def stacked(buf, s, first, heads):
        cols = [buf[4 * s : 4 * s + 4, :, pl.ds(pl.multiple_of(first + h * HD, HD), HD)].reshape(LR, HD) for h in range(heads)]
        return jnp.concatenate(cols, axis=0)

    def hand_over(kv, s, grad):
        out = grad.astype(BF)
        compact[kv][0, s] = out[:PL].reshape(BLOCKS, BR, HD)
        rgbuf[4 * s : 4 * s + 4, :, kv * HD : (kv + 1) * HD] = out[PL:].reshape(4, 16, HD)
        send(compact[kv].at[0, s], compact[kv].at[1, s], cc_s.at[kv], cc_r.at[kv], other_core)

    wait(table[K].at[:, 1], agc_r.at[K])
    for s in range(SLOTS):
        pick(kcat, K, s)
        n, keys = length[s], kcat[s]

        def first_pass(h, _, s=s, n=n, keys=keys):
            q = stacked(qbuf, s, h * HALF * HD, HALF)
            scores = dot(keys, q, ((1,), (1,))) * SCALE
            u = lax.broadcasted_iota(jnp.int32, (LR, WIDE), 0)
            at = lax.rem(lax.broadcasted_iota(jnp.int32, (LR, WIDE), 1), LR)
            own_scores = jnp.where((u <= at) & (u < n), scores[PL:], -jnp.inf)
            scores = jnp.concatenate([scores[:PL], own_scores], axis=0)
            top = jnp.max(scores, axis=0, keepdims=True)
            e = jnp.exp(scores - top)
            probs = e * (1.0 / jnp.sum(e, axis=0, keepdims=True))
            cols = columns(WIDE, h)
            probs_f[s, :, cols] = probs
            probs_t[s, :, cols] = probs.astype(BF)
            return 0

        lax.fori_loop(0, 2, first_pass, 0, unroll=True)
        hand_over(V, s, dot(probs_t[s], stacked(gbuf, s, 0, GROUP), ((1,), (0,))))

    learner2 = dp + 1 - 2 * core
    slot_prompts = prompt + [lax.div(lists[s, learner2], G) for s in range(SLOTS)]

    def fill(kv, first, count):
        def one(i, _):
            k = lax.rem(first + i, Z)
            for a in range(2):
                code = owners[(y + a - 2 * a * y) * (2 * Z) + lax.rem(z + way * (k - 8) + Z, Z) * 2 + core]
                p, b = lax.div(code, BLOCKS), lax.rem(code, BLOCKS)
                total = jnp.zeros((BR, HD), F32)
                for c in range(2):
                    for s in range(SLOTS):
                        hit = slot_prompts[c * SLOTS + s] == p
                        total = total + jnp.where(hit, compact[kv][c, s, b].astype(F32), 0.0)
                part[kv, a, k] = total.astype(BF)
            return 0

        if count == 1:
            one(0, 0)
        else:
            lax.fori_loop(0, count, one, 0)

    def far(kv):
        wait(compact[kv].at[1], cc_r.at[kv])
        for i, d in enumerate((4, 3, 2, 1)):
            fill(kv, (8 + d + 4) % Z, 1)
            send(part.at[kv, :, (8 + d + 4) % Z], relay_a.at[kv, i], rs_s.at[kv, 0], rs_r.at[kv, 0], at(0, d))
        for i, d in enumerate((-3, -2, -1)):
            fill(kv, 8 + d - 4, 1)
            send(part.at[kv, :, 8 + d - 4], relay_b.at[kv, i], rs_s.at[kv, 0], rs_r.at[kv, 1], at(0, d))

    near_slots = pl.ds(5, 7)

    def near_y(kv):
        fill(kv, 4, 9)
        send(part.at[kv, 1, near_slots], ypart.at[kv], rs_s.at[kv, 1], rs_r.at[kv, 2], at(1, 0))

    def near_z(kv):
        wait(ypart.at[kv], rs_r.at[kv, 2])
        part[kv, 0, near_slots] = (part[kv, 0, near_slots].astype(F32) + ypart[kv].astype(F32)).astype(BF)
        for i, d in enumerate(NEAR[2:]):
            send(part.at[kv, 0, 8 + d], direct.at[kv, i], rs_s.at[kv, 2], rs_r.at[kv, 3], at(0, d))

    def relay(kv):
        for j, (slot, buf, count) in enumerate(((12, relay_a, 4), (4, relay_b, 3))):
            wait(buf.at[kv], rs_r.at[kv, j])
            total = part[kv, :, slot].astype(F32)
            for i in range(count):
                total = total + buf[kv, i].astype(F32)
            part[kv, :, slot] = total.astype(BF)
            for a in (1, 0):
                send(part.at[kv, a, slot], relayed.at[kv, 2 * j + a], rs_s.at[kv, 3], rs_r.at[kv, 4], at(a, slot - 8))

    def finish(kv):
        wait(direct.at[kv], rs_r.at[kv, 3])
        total = part[kv, 0, 8].astype(F32)
        for i in range(6):
            total = total + direct[kv, i].astype(F32)
        wait(relayed.at[kv], rs_r.at[kv, 4])
        for i in range(4):
            total = total + relayed[kv, i].astype(F32)
        pg_out[:, kv * HD : (kv + 1) * HD] = total.astype(BF)

    wait(table[V].at[:, 1], agc_r.at[V])
    for s in range(SLOTS):
        pick(vcat, V, s)
        values = vcat[s]

        def second_pass(h, _, s=s, values=values):
            g = stacked(gbuf, s, h * HALF * HD, HALF)
            cols = columns(WIDE, h)
            dprob = dot(values, g, ((1,), (1,)))
            delta = jnp.sum(probs_t[s, :, cols].astype(F32) * dprob, axis=0, keepdims=True)
            dscore_t[s, :, cols] = (probs_f[s, :, cols] * (dprob - delta) * SCALE).astype(BF)
            return 0

        lax.fori_loop(0, 2, second_pass, 0, unroll=True)
        hand_over(K, s, dot(dscore_t[s], stacked(qbuf, s, 0, GROUP), ((1,), (0,))))
        if s == 0:
            far(V)
            near_y(V)

    results = ((obuf, att_out, HW), (dqbuf, qg_out, HW), (rgbuf, rg_out, KW))

    def to_rows(a):
        src, to, width = results[a]
        for p in peers:
            send(src.at[p], to.at[:, columns(width, t)], back_s.at[a], back_r.at[a], (dp, p))
        copy = pltpu.make_async_copy(src.at[t], to.at[:, columns(width, t)], loc.at[a])
        copy.start()
        return copy

    def back(a, left, right):
        for s in range(SLOTS):
            for h in range(2):
                rows = dot(left[s, :, h * WIDE : (h + 1) * WIDE], right[s], ((0,), (0,)))
                for i in range(HALF):
                    head = slice((h * HALF + i) * HD, (h * HALF + i + 1) * HD)
                    values = rows[i * LR : (i + 1) * LR]
                    if a == 0:
                        live = lax.broadcasted_iota(jnp.int32, (LR, HD), 0) < length[s]
                        values = jnp.where(live, values, 0.0)
                    results[a][0][4 * s : 4 * s + 4, :, head] = values.astype(BF).reshape(4, 16, HD)

    far(K)
    near_y(K)
    back(0, probs_t, vcat)
    near_z(V)
    near_z(K)
    stay = [to_rows(0)]
    relay(V)
    back(1, dscore_t, kcat)
    relay(K)
    stay.append(to_rows(2))
    stay.append(to_rows(1))
    finish(V)
    finish(K)

    for a, (buf, _, _) in enumerate(results):
        wait(buf.at[pl.ds(0, T - 1)], back_r.at[a])
        wait(buf.at[pl.ds(0, T - 1)], back_s.at[a])
    for copy in stay:
        copy.wait()
    for a, buf in enumerate((kvbuf, qbuf, gbuf)):
        wait(buf.at[pl.ds(0, T - 1)], a2a_s.at[a])
    for kv in (K, V):
        wait(table[kv].at[:, 0, pl.ds(0, 11)], agz_s.at[kv])
        wait(table[kv].at[0, 0, near], agy_s.at[kv])
        wait(table[kv].at[:, 0], agc_s.at[kv])
        wait(compact[kv].at[0], cc_s.at[kv])
        wait(part.at[kv, :, pl.ds(0, 7)], rs_s.at[kv, 0])
        wait(ypart.at[kv], rs_s.at[kv, 1])
        wait(direct.at[kv], rs_s.at[kv, 2])
        wait(relayed.at[kv], rs_s.at[kv, 3])


def hand_on(*refs):
    copies = [pltpu.make_async_copy(refs[i], refs[4 + i], refs[8].at[i]) for i in range(4)]
    for copy in copies:
        copy.start()
    for copy in copies:
        copy.wait()


def on_device(resp_q, resp_kv, prompt_kv, grad_out, lengths, resp_lists, owner_map):
    anywhere = pl.BlockSpec(memory_space=pl.ANY)
    in_vmem = pl.BlockSpec(memory_space=pltpu.VMEM)
    rows = resp_q.shape[0]
    dma = pltpu.SemaphoreType.DMA
    results = pl.pallas_call(
        kernel,
        name="attention",
        out_shape=(
            pltpu.VMEM(resp_q.shape, BF),
            pltpu.VMEM(resp_q.shape, BF),
            pltpu.VMEM(resp_kv.shape, BF),
            pltpu.VMEM(prompt_kv.shape, BF),
        ),
        in_specs=[anywhere] * 7,
        out_specs=(in_vmem,) * 4,
        scratch_shapes=[
            pltpu.VMEM((T, rows, HW), BF),
            pltpu.VMEM((T, rows, HW), BF),
            pltpu.VMEM((T, rows, KW), BF),
            pltpu.VMEM((T, rows, HW), BF),
            pltpu.VMEM((T, rows, HW), BF),
            pltpu.VMEM((T, rows, KW), BF),
            pltpu.VMEM((2, 2, Z, BR, HD), BF),
            pltpu.VMEM((2, 2, Z, BR, HD), BF),
            pltpu.VMEM((SLOTS, KEYS, HD), BF),
            pltpu.VMEM((SLOTS, KEYS, HD), BF),
            pltpu.VMEM((SLOTS, KEYS, GROUP * LR), F32),
            pltpu.VMEM((SLOTS, KEYS, GROUP * LR), BF),
            pltpu.VMEM((SLOTS, KEYS, GROUP * LR), BF),
            pltpu.VMEM((2, SLOTS, BLOCKS, BR, HD), BF),
            pltpu.VMEM((2, SLOTS, BLOCKS, BR, HD), BF),
            pltpu.VMEM((2, 2, Z, BR, HD), BF),
            pltpu.VMEM((2, 6, BR, HD), BF),
            pltpu.VMEM((2, 4, 2, BR, HD), BF),
            pltpu.VMEM((2, 3, 2, BR, HD), BF),
            pltpu.VMEM((2, 4, BR, HD), BF),
            pltpu.VMEM((2, 7, BR, HD), BF),
            pltpu.SMEM(lengths.shape, jnp.int32),
            pltpu.SMEM(resp_lists.shape[::-1], jnp.int32),
            pltpu.SMEM(owner_map.shape, jnp.int32),
            dma((8,)),
            dma((3,)),
            dma((3,)),
            dma((2,)),
            dma((2, 7)),
            dma((2,)),
            dma((2,)),
            dma((2,)),
            dma((2,)),
            dma((3,)),
            dma((3,)),
            dma((2,)),
            dma((2,)),
            dma((2, 4)),
            dma((2, 5)),
            pltpu.SemaphoreType.REGULAR,
        ],
        compiler_params=pltpu.CompilerParams(
            collective_id=0, has_side_effects=True, vmem_limit_bytes=60 * 1024 * 1024
        ),
    )(resp_q, resp_kv, prompt_kv, grad_out, lengths, resp_lists.T, owner_map)
    return pl.pallas_call(
        hand_on,
        name="hand_on",
        out_shape=tuple(jax.ShapeDtypeStruct(r.shape, r.dtype) for r in results),
        in_specs=[in_vmem] * 4,
        out_specs=(anywhere,) * 4,
        scratch_shapes=[dma((4,))],
    )(*[pltpu.with_memory_space_constraint(r, pltpu.VMEM) for r in results])


def solution(mesh):
    rows = P(("dp", "tensor"), None)
    return jax.shard_map(
        on_device,
        mesh=mesh,
        in_specs=(rows, rows, P("dp", "tensor"), rows, P(), P(), P()),
        out_specs=(rows, rows, rows, P("dp", "tensor")),
        check_vma=False,
    )
```

```python
import math

import jax
import jax.numpy as jnp
from jax import lax
from jax.experimental import pallas as pl
from jax.experimental.pallas import tpu as pltpu
from jax.sharding import PartitionSpec as P

MESH = pl.DeviceIdType.MESH
BF = jnp.bfloat16
F32 = jnp.float32
HD = 128
BLOCKS = 8
G = 16
Z = 16
T = 8
SLOTS = 2
LR = 64
GROUP = 8
BR = 32
PL = BLOCKS * BR
KEYS = PL + LR
HW = GROUP * HD
KW = 2 * HD
HALF = GROUP // 2
WIDE = HALF * LR
SCALE = 1.0 / math.sqrt(HD)
NEAR = (4, -4, 3, -3, 2, -2, 1, -1)
K, V = 0, 1


def dot(a, b, dims):
    return lax.dot_general(a, b, (dims, ((), ())), preferred_element_type=F32)


def kernel(
    q_in, kv_in, pkv_in, g_in, lengths_in, lists_in, owners_in,
    att_out, qg_out, rg_out, pg_out,
    qbuf, gbuf, kvbuf, obuf, dqbuf, rgbuf,
    table_k, table_v, kcat, vcat, probs_t, dscore_t,
    compact_k, compact_v, part, direct, relay_a, relay_b, relayed, ypart, lengths, lists, owners,
    loc, a2a_s, a2a_r, agz_s, agz_r, agy_s, agy_r, agc_s, agc_r, back_s, back_r, cc_s, cc_r, rs_s, rs_r, heard,
):
    table, compact = (table_k, table_v), (compact_k, compact_v)
    dp = lax.axis_index("dp")
    t = lax.axis_index("tensor")
    core = lax.rem(dp, 2)
    z = lax.rem(dp // 2, Z)
    y = dp // (2 * Z)

    way = 1 - 2 * core

    def at(a, d):
        return ((y + a - 2 * a * y) * (2 * Z) + lax.rem(z + way * d + Z, Z) * 2 + core, t)

    other_core = (y * (2 * Z) + z * 2 + (1 - core), t)
    peers = [lax.rem(t + k, T) for k in range(1, T)]

    def send(src, dst, s, r, device):
        pltpu.make_async_remote_copy(
            src_ref=src, dst_ref=dst, send_sem=s, recv_sem=r, device_id=device, device_id_type=MESH
        ).start()

    def wait(ref, sem):
        pltpu.make_async_copy(ref, ref, sem).wait()

    def columns(width, index):
        return pl.ds(pl.multiple_of(index * width, width), width)

    barrier = pltpu.get_barrier_semaphore()
    greeted = [(dp, p) for p in peers] + [at(0, d) for d in NEAR] + [at(1, 0), other_core]
    for device in greeted:
        pl.semaphore_signal(barrier, inc=1, device_id=device, device_id_type=MESH)
    local = [
        pltpu.make_async_copy(pkv_in.at[:, :HD], table[K].at[0, 0, 8], loc.at[0]),
        pltpu.make_async_copy(pkv_in.at[:, HD:], table[V].at[0, 0, 8], loc.at[1]),
        pltpu.make_async_copy(kv_in.at[:, columns(KW, t)], kvbuf.at[t], loc.at[2]),
        pltpu.make_async_copy(q_in.at[:, columns(HW, t)], qbuf.at[t], loc.at[3]),
        pltpu.make_async_copy(g_in.at[:, columns(HW, t)], gbuf.at[t], loc.at[4]),
        pltpu.make_async_copy(lengths_in, lengths, loc.at[5]),
        pltpu.make_async_copy(lists_in, lists, loc.at[6]),
        pltpu.make_async_copy(owners_in, owners, loc.at[7]),
    ]
    for copy in local:
        copy.start()
    for copy in local[:2]:
        copy.wait()
    pl.semaphore_wait(barrier, len(greeted))
    pl.semaphore_signal(heard, inc=1, device_id=at(1, 0), device_id_type=MESH)

    def arrival(a, slot):
        return 0 if slot == 4 else 1 if slot == 12 else 2 if 4 < slot < 12 else 3 + 2 * a if slot < 4 else 4 + 2 * a

    def gather(kv, a, slot, d):
        to = slot - d
        send(table[kv].at[0, 0, slot], table[kv].at[a, 0, to], agz_s.at[kv], agz_r.at[kv, arrival(a, to)], at(a, d))

    def to_heads(a, src, dst, width):
        for p in peers:
            send(src.at[:, columns(width, p)], dst.at[t], a2a_s.at[a], a2a_r.at[a], (dp, p))

    for d in NEAR:
        gather(K, 0, 8, d)
    for d in NEAR:
        gather(V, 0, 8, d)
    to_heads(0, kv_in, kvbuf, KW)
    to_heads(1, q_in, qbuf, HW)
    to_heads(2, g_in, gbuf, HW)

    pl.semaphore_wait(heard, 1)
    for kv in (K, V):
        wait(table[kv].at[0, 0, 4], agz_r.at[kv, 0])
        for d in (4, 3, 2, 1):
            for a in (1, 0):
                gather(kv, a, 4, d)
        wait(table[kv].at[0, 0, 12], agz_r.at[kv, 1])
        for d in (-3, -2, -1):
            for a in (1, 0):
                gather(kv, a, 12, d)

    groups = (pl.ds(4, 9), pl.ds(0, 4), pl.ds(13, 3))

    def over_core(kv, a, i):
        r = groups[i]
        send(table[kv].at[a, 0, r], table[kv].at[a, 1, r], agc_s.at[kv], agc_r.at[kv], other_core)

    for kv in (K, V):
        wait(table[kv].at[0, 0, pl.ds(4, 6)], agz_r.at[kv, 2])
        near = groups[0]
        send(table[kv].at[0, 0, near], table[kv].at[1, 0, near], agy_s.at[kv], agy_r.at[kv], at(1, 0))
        over_core(kv, 0, 0)

    for copy in local[5:]:
        copy.wait()
    resp = [lists[s, dp] for s in range(SLOTS)]
    prompt = [lax.div(a, G) for a in resp]
    length = [lengths[a] for a in resp]

    def find(j, found):
        code = owners[j]
        return tuple(
            jnp.where(code == prompt[s] * BLOCKS + b, j, found[s * BLOCKS + b])
            for s in range(SLOTS)
            for b in range(BLOCKS)
        )

    found = lax.fori_loop(0, 4 * Z, find, tuple(jnp.int32(0) for _ in range(SLOTS * BLOCKS)), unroll=4)

    def pick(cat, kv, s):
        for b in range(BLOCKS):
            j = found[s * BLOCKS + b]
            jy, jz, jc = lax.div(j, 2 * Z), lax.rem(lax.div(j, 2), Z), lax.rem(j, 2)
            slot = lax.rem((1 - 2 * jc) * (jz - z) + 8 + Z, Z)
            block = table[kv][jnp.where(jy == y, 0, 1), jnp.where(jc == core, 0, 1), slot]
            cat[s, b * BR : (b + 1) * BR] = block

    for kv in (K, V):
        wait(table[kv].at[1, 0, groups[0]], agy_r.at[kv])
        over_core(kv, 1, 0)
        for i in (1, 2):
            for a in range(2):
                wait(table[kv].at[a, 0, groups[i]], agz_r.at[kv, 2 + i + 2 * a])
                over_core(kv, a, i)
    for copy in local[2:5]:
        copy.wait()
    for a, buf in enumerate((kvbuf, qbuf, gbuf)):
        wait(buf.at[pl.ds(0, T - 1)], a2a_r.at[a])
    for s in range(SLOTS):
        row = lax.broadcasted_iota(jnp.int32, (LR, HW), 0)
        masked = jnp.where(row < length[s], gbuf[4 * s : 4 * s + 4].reshape(LR, HW).astype(F32), 0.0)
        gbuf[4 * s : 4 * s + 4] = masked.astype(BF).reshape(4, 16, HW)
        own = kvbuf[4 * s : 4 * s + 4].reshape(LR, KW)
        kcat[s, PL:] = own[:, :HD]
        vcat[s, PL:] = own[:, HD:]

    def stacked(buf, s, first, heads):
        cols = [buf[4 * s : 4 * s + 4, :, pl.ds(pl.multiple_of(first + h * HD, HD), HD)].reshape(LR, HD) for h in range(heads)]
        return jnp.concatenate(cols, axis=0)

    def hand_over(kv, s, grad):
        out = grad.astype(BF)
        compact[kv][0, s] = out[:PL].reshape(BLOCKS, BR, HD)
        rgbuf[4 * s : 4 * s + 4, :, kv * HD : (kv + 1) * HD] = out[PL:].reshape(4, 16, HD)
        send(compact[kv].at[0, s], compact[kv].at[1, s], cc_s.at[kv], cc_r.at[kv], other_core)

    wait(table[K].at[:, 1], agc_r.at[K])
    for s in range(SLOTS):
        pick(kcat, K, s)
        n, keys = length[s], kcat[s]

        def first_pass(h, _, s=s, n=n, keys=keys):
            q = stacked(qbuf, s, h * HALF * HD, HALF)
            scores = dot(keys, q, ((1,), (1,))) * SCALE
            u = lax.broadcasted_iota(jnp.int32, (LR, WIDE), 0)
            at = lax.rem(lax.broadcasted_iota(jnp.int32, (LR, WIDE), 1), LR)
            own_scores = jnp.where((u <= at) & (u < n), scores[PL:], -jnp.inf)
            scores = jnp.concatenate([scores[:PL], own_scores], axis=0)
            top = jnp.max(scores, axis=0, keepdims=True)
            e = jnp.exp(scores - top)
            probs = e * (1.0 / jnp.sum(e, axis=0, keepdims=True))
            cols = columns(WIDE, h)
            probs_t[s, :, cols] = probs.astype(BF)
            return 0

        lax.fori_loop(0, 2, first_pass, 0, unroll=True)
        hand_over(V, s, dot(probs_t[s], stacked(gbuf, s, 0, GROUP), ((1,), (0,))))

    learner2 = dp + 1 - 2 * core
    slot_prompts = prompt + [lax.div(lists[s, learner2], G) for s in range(SLOTS)]

    def fill(kv, first, count):
        def one(i, _):
            k = lax.rem(first + i, Z)
            for a in range(2):
                code = owners[(y + a - 2 * a * y) * (2 * Z) + lax.rem(z + way * (k - 8) + Z, Z) * 2 + core]
                p, b = lax.div(code, BLOCKS), lax.rem(code, BLOCKS)
                total = jnp.zeros((BR, HD), F32)
                for c in range(2):
                    for s in range(SLOTS):
                        hit = slot_prompts[c * SLOTS + s] == p
                        total = total + jnp.where(hit, compact[kv][c, s, b].astype(F32), 0.0)
                part[kv, a, k] = total.astype(BF)
            return 0

        if count == 1:
            one(0, 0)
        else:
            lax.fori_loop(0, count, one, 0)

    def far(kv):
        wait(compact[kv].at[1], cc_r.at[kv])
        for i, d in enumerate((4, 3, 2, 1)):
            fill(kv, (8 + d + 4) % Z, 1)
            send(part.at[kv, :, (8 + d + 4) % Z], relay_a.at[kv, i], rs_s.at[kv, 0], rs_r.at[kv, 0], at(0, d))
        for i, d in enumerate((-3, -2, -1)):
            fill(kv, 8 + d - 4, 1)
            send(part.at[kv, :, 8 + d - 4], relay_b.at[kv, i], rs_s.at[kv, 0], rs_r.at[kv, 1], at(0, d))

    near_slots = pl.ds(5, 7)

    def near_y(kv):
        fill(kv, 4, 9)
        send(part.at[kv, 1, near_slots], ypart.at[kv], rs_s.at[kv, 1], rs_r.at[kv, 2], at(1, 0))

    def near_z(kv):
        wait(ypart.at[kv], rs_r.at[kv, 2])
        part[kv, 0, near_slots] = (part[kv, 0, near_slots].astype(F32) + ypart[kv].astype(F32)).astype(BF)
        for i, d in enumerate(NEAR[2:]):
            send(part.at[kv, 0, 8 + d], direct.at[kv, i], rs_s.at[kv, 2], rs_r.at[kv, 3], at(0, d))

    def relay(kv):
        for j, (slot, buf, count) in enumerate(((12, relay_a, 4), (4, relay_b, 3))):
            wait(buf.at[kv], rs_r.at[kv, j])
            total = part[kv, :, slot].astype(F32)
            for i in range(count):
                total = total + buf[kv, i].astype(F32)
            part[kv, :, slot] = total.astype(BF)
            for a in (1, 0):
                send(part.at[kv, a, slot], relayed.at[kv, 2 * j + a], rs_s.at[kv, 3], rs_r.at[kv, 4], at(a, slot - 8))

    def finish(kv):
        wait(direct.at[kv], rs_r.at[kv, 3])
        total = part[kv, 0, 8].astype(F32)
        for i in range(6):
            total = total + direct[kv, i].astype(F32)
        wait(relayed.at[kv], rs_r.at[kv, 4])
        for i in range(4):
            total = total + relayed[kv, i].astype(F32)
        pg_out[:, kv * HD : (kv + 1) * HD] = total.astype(BF)

    wait(table[V].at[:, 1], agc_r.at[V])
    for s in range(SLOTS):
        pick(vcat, V, s)
        values = vcat[s]

        def second_pass(h, _, s=s, values=values):
            g = stacked(gbuf, s, h * HALF * HD, HALF)
            cols = columns(WIDE, h)
            dprob = dot(values, g, ((1,), (1,)))
            probs = probs_t[s, :, cols].astype(F32)
            delta = jnp.sum(probs * dprob, axis=0, keepdims=True)
            dscore_t[s, :, cols] = (probs * (dprob - delta) * SCALE).astype(BF)
            return 0

        lax.fori_loop(0, 2, second_pass, 0, unroll=True)
        hand_over(K, s, dot(dscore_t[s], stacked(qbuf, s, 0, GROUP), ((1,), (0,))))
        if s == 0:
            far(V)

    results = ((obuf, att_out, HW), (dqbuf, qg_out, HW), (rgbuf, rg_out, KW))

    def to_rows(a):
        src, to, width = results[a]
        for p in peers:
            send(src.at[p], to.at[:, columns(width, t)], back_s.at[a], back_r.at[a], (dp, p))
        copy = pltpu.make_async_copy(src.at[t], to.at[:, columns(width, t)], loc.at[a])
        copy.start()
        return copy

    def back(a, left, right):
        for s in range(SLOTS):
            for h in range(2):
                rows = dot(left[s, :, h * WIDE : (h + 1) * WIDE], right[s], ((0,), (0,)))
                for i in range(HALF):
                    head = slice((h * HALF + i) * HD, (h * HALF + i + 1) * HD)
                    values = rows[i * LR : (i + 1) * LR]
                    if a == 0:
                        live = lax.broadcasted_iota(jnp.int32, (LR, HD), 0) < length[s]
                        values = jnp.where(live, values, 0.0)
                    results[a][0][4 * s : 4 * s + 4, :, head] = values.astype(BF).reshape(4, 16, HD)

    far(K)
    near_y(V)
    near_y(K)
    back(0, probs_t, vcat)
    near_z(V)
    near_z(K)
    stay = [to_rows(0)]
    relay(V)
    back(1, dscore_t, kcat)
    relay(K)
    stay.append(to_rows(2))
    stay.append(to_rows(1))
    finish(V)
    finish(K)

    for a, (buf, _, _) in enumerate(results):
        wait(buf.at[pl.ds(0, T - 1)], back_r.at[a])
        wait(buf.at[pl.ds(0, T - 1)], back_s.at[a])
    for copy in stay:
        copy.wait()
    for a, buf in enumerate((kvbuf, qbuf, gbuf)):
        wait(buf.at[pl.ds(0, T - 1)], a2a_s.at[a])
    for kv in (K, V):
        wait(table[kv].at[:, 0, pl.ds(0, 11)], agz_s.at[kv])
        wait(table[kv].at[0, 0, near], agy_s.at[kv])
        wait(table[kv].at[:, 0], agc_s.at[kv])
        wait(compact[kv].at[0], cc_s.at[kv])
        wait(part.at[kv, :, pl.ds(0, 7)], rs_s.at[kv, 0])
        wait(ypart.at[kv], rs_s.at[kv, 1])
        wait(direct.at[kv], rs_s.at[kv, 2])
        wait(relayed.at[kv], rs_s.at[kv, 3])


def hand_on(*refs):
    copies = [pltpu.make_async_copy(refs[i], refs[4 + i], refs[8].at[i]) for i in range(4)]
    for copy in copies:
        copy.start()
    for copy in copies:
        copy.wait()


def on_device(resp_q, resp_kv, prompt_kv, grad_out, lengths, resp_lists, owner_map):
    anywhere = pl.BlockSpec(memory_space=pl.ANY)
    in_vmem = pl.BlockSpec(memory_space=pltpu.VMEM)
    rows = resp_q.shape[0]
    dma = pltpu.SemaphoreType.DMA
    results = pl.pallas_call(
        kernel,
        name="attention",
        out_shape=(
            pltpu.VMEM(resp_q.shape, BF),
            pltpu.VMEM(resp_q.shape, BF),
            pltpu.VMEM(resp_kv.shape, BF),
            pltpu.VMEM(prompt_kv.shape, BF),
        ),
        in_specs=[anywhere] * 7,
        out_specs=(in_vmem,) * 4,
        scratch_shapes=[
            pltpu.VMEM((T, rows, HW), BF),
            pltpu.VMEM((T, rows, HW), BF),
            pltpu.VMEM((T, rows, KW), BF),
            pltpu.VMEM((T, rows, HW), BF),
            pltpu.VMEM((T, rows, HW), BF),
            pltpu.VMEM((T, rows, KW), BF),
            pltpu.VMEM((2, 2, Z, BR, HD), BF),
            pltpu.VMEM((2, 2, Z, BR, HD), BF),
            pltpu.VMEM((SLOTS, KEYS, HD), BF),
            pltpu.VMEM((SLOTS, KEYS, HD), BF),
            pltpu.VMEM((SLOTS, KEYS, GROUP * LR), BF),
            pltpu.VMEM((SLOTS, KEYS, GROUP * LR), BF),
            pltpu.VMEM((2, SLOTS, BLOCKS, BR, HD), BF),
            pltpu.VMEM((2, SLOTS, BLOCKS, BR, HD), BF),
            pltpu.VMEM((2, 2, Z, BR, HD), BF),
            pltpu.VMEM((2, 6, BR, HD), BF),
            pltpu.VMEM((2, 4, 2, BR, HD), BF),
            pltpu.VMEM((2, 3, 2, BR, HD), BF),
            pltpu.VMEM((2, 4, BR, HD), BF),
            pltpu.VMEM((2, 7, BR, HD), BF),
            pltpu.SMEM(lengths.shape, jnp.int32),
            pltpu.SMEM(resp_lists.shape[::-1], jnp.int32),
            pltpu.SMEM(owner_map.shape, jnp.int32),
            dma((8,)),
            dma((3,)),
            dma((3,)),
            dma((2,)),
            dma((2, 7)),
            dma((2,)),
            dma((2,)),
            dma((2,)),
            dma((2,)),
            dma((3,)),
            dma((3,)),
            dma((2,)),
            dma((2,)),
            dma((2, 4)),
            dma((2, 5)),
            pltpu.SemaphoreType.REGULAR,
        ],
        compiler_params=pltpu.CompilerParams(
            collective_id=0, has_side_effects=True, vmem_limit_bytes=60 * 1024 * 1024
        ),
    )(resp_q, resp_kv, prompt_kv, grad_out, lengths, resp_lists.T, owner_map)
    return pl.pallas_call(
        hand_on,
        name="hand_on",
        out_shape=tuple(jax.ShapeDtypeStruct(r.shape, r.dtype) for r in results),
        in_specs=[in_vmem] * 4,
        out_specs=(anywhere,) * 4,
        scratch_shapes=[dma((4,))],
    )(*[pltpu.with_memory_space_constraint(r, pltpu.VMEM) for r in results])


def solution(mesh):
    rows = P(("dp", "tensor"), None)
    return jax.shard_map(
        on_device,
        mesh=mesh,
        in_specs=(rows, rows, P("dp", "tensor"), rows, P(), P(), P()),
        out_specs=(rows, rows, rows, P("dp", "tensor")),
        check_vma=False,
    )
```
